32 devices in a mesh: row: 8 (over y, x, core), col: 4 (over z).
Axes of the slice: x: 2, y: 2, z: 4, core: 2. Of those that a mesh axis runs over, the one named last changes fastest.
Arguments:
- single: float32 [512, 768], P('row', 'col'), may hold values from -6 to 6
- pair: float32 [512, 512, 128], P('row', 'col'), may hold values from -6 to 6
- single_gain: float32 [768], replicated, may hold values from 0.25 to 1.75
- pair_gain: float32 [128], replicated, may hold values from 0.25 to 1.75
- w_query: float32 [768, 768], replicated, may hold values from -0.25 to 0.25
- w_key: float32 [768, 768], replicated, may hold values from -0.25 to 0.25
- w_value: float32 [768, 768], replicated, may hold values from -0.21875 to 0.21875
- w_gate: float32 [768, 768], replicated, may hold values from -0.21875 to 0.21875
- w_bias: float32 [128, 16], replicated, may hold values from -0.5 to 0.5
- w_out: float32 [768, 768], P(None, 'col'), may hold values from -0.21875 to 0.21875
- cotangent: float32 [512, 768], P('row', 'col'), may hold values from -6 to 6
Outputs:
- attended: float32 [512, 768], P('row', 'col')
- pair_grad: float32 [512, 512, 128], P('row', 'col')
- bias_grad: float32 [128, 16], replicated
The draws below stay inside these ranges and needn't reach their ends.
All inputs are finite; a program needn't handle non-finite values.
Results may differ from the reference program's by a relative error of at most 0.0003.
Values sent between devices are 32-bit elements; how exact they have to be, the bound alone decides.
A program may use at most 128 MiB of HBM per device.

```python
import jax
import jax.numpy as jnp
from jax import lax

D = 768
HEADS = 16
PAIR_C = 128
TR = 64
TOKENS = 512
N_ROW = 8


def projection(key, salt):
    key = jax.random.fold_in(key, salt)
    matrix = jax.random.normal(key, (D, D), jnp.float32) * D ** (-0.5)
    matrix = jnp.clip(matrix, -6.0 * D ** (-0.5), 6.0 * D ** (-0.5))
    return jnp.clip(matrix, -0.25, 0.25)


def draw_single(key, part):
    key = jax.random.fold_in(key, 11)
    base = jax.random.normal(key, (TOKENS, D), jnp.float32)
    return jnp.clip(base, -6.0, 6.0)


def draw_w_query(key, part):
    return projection(key, 23)


def draw_w_key(key, part):
    return projection(key, 37)


def block_scale(key, dims, pieces, smallest, top_value):
    def one(position, blocks):
        heights = jax.random.uniform(jax.random.fold_in(jax.random.fold_in(key, 6), position), (blocks,), jnp.float32, smallest / len(pieces), top_value / len(pieces))
        return jnp.repeat(jnp.exp(heights), dims[position] // blocks).reshape((-1,) + (1,) * (len(dims) - position - 1))

    loudness = one(*pieces[0])
    for cut in pieces[1:]:
        loudness = loudness * one(*cut)
    return loudness


def scatter_about(stream_key, shape, scale, reach, pieces=(), held_as=jnp.bfloat16):
    level = block_scale(stream_key, shape, pieces, -0.22, 0.18) if pieces else 1.0
    drawn = jax.random.normal(stream_key, shape, jnp.float32) * scale * level
    return jnp.minimum(jnp.maximum(drawn, -reach), reach).astype(held_as)


def setup_inputs(seed: int = 0) -> dict:
    seeds = jax.random.split(jax.random.key(seed), 12)
    single = draw_single(jax.random.fold_in(seeds[11], 71), 0)
    pair = scatter_about(seeds[1], (TOKENS, TOKENS, PAIR_C), 1.0, 6.0, ((0, 8), (1, 4)), jnp.float32)
    single_gain = jnp.clip(1.0 + 0.15 * jax.random.normal(seeds[2], (D,), jnp.float32), 0.25, 1.75)
    pair_gain = jnp.clip(1.0 + 0.15 * jax.random.normal(seeds[3], (PAIR_C,), jnp.float32), 0.25, 1.75)
    w_query = draw_w_query(jax.random.fold_in(seeds[11], 71), 0)
    w_key = draw_w_key(jax.random.fold_in(seeds[11], 71), 0)
    w_value = scatter_about(seeds[6], (D, D), D ** -0.5, 0.21875, (), jnp.float32)
    w_gate = scatter_about(seeds[7], (D, D), D ** -0.5, 0.21875, (), jnp.float32)
    w_bias = scatter_about(seeds[8], (PAIR_C, HEADS), PAIR_C ** -0.5, 0.5, (), jnp.float32)
    w_out = scatter_about(seeds[9], (D, D), D ** -0.5, 0.21875, ((1, 4),), jnp.float32)
    cotangent = scatter_about(seeds[10], (TOKENS, D), 1.0, 6.0, ((0, 8), (1, 4)), jnp.float32)
    return dict(single=single, pair=pair, single_gain=single_gain, pair_gain=pair_gain, w_query=w_query, w_key=w_key, w_value=w_value, w_gate=w_gate, w_bias=w_bias, w_out=w_out, cotangent=cotangent)


def layer_norm(values_in, gain):
    centre = lax.optimization_barrier(jnp.mean(values_in, axis=-1, keepdims=True))
    spread = lax.optimization_barrier(jnp.mean((values_in - centre) ** 2, axis=-1, keepdims=True))
    return (values_in - centre) * lax.rsqrt(spread + 1e-05) * gain

def reference(single, pair, single_gain, pair_gain, w_query, w_key, w_value, w_gate, w_bias, w_out, cotangent):
    highest = lax.Precision.HIGHEST
    head_dim = D // HEADS
    normed = layer_norm(single, single_gain)
    query = jnp.dot(normed, w_query, precision=highest).reshape(TOKENS, HEADS, head_dim)
    keys = jnp.dot(normed, w_key, precision=highest).reshape(TOKENS, HEADS, head_dim)
    values = jnp.dot(normed, w_value, precision=highest).reshape(TOKENS, HEADS, head_dim)
    gating = jax.nn.sigmoid(jnp.dot(normed, w_gate, precision=highest))
    scale = head_dim ** (-0.5)

    def bias_of(pair_rows, weight):
        return jnp.einsum('ijc,ch->ihj', layer_norm(pair_rows, pair_gain), weight, precision=highest)

    def weights_of(index):
        start = (index * TR).astype(jnp.int32)
        query_rows = lax.dynamic_slice_in_dim(query, start, TR, 0)
        pair_rows = lax.dynamic_slice_in_dim(pair, start, TR, 0)
        scores = jnp.einsum('ihd,jhd->ihj', query_rows, keys, precision=highest) * scale + bias_of(pair_rows, w_bias)
        return (jax.nn.softmax(scores, axis=-1), pair_rows)

    def forward_block(index):
        soft_weights, _ = weights_of(index)
        return jnp.einsum('ihj,jhd->ihd', soft_weights, values, precision=highest)
    blocks = jnp.arange(N_ROW, dtype=jnp.int32)
    context = lax.map(forward_block, blocks).reshape(TOKENS, D)
    attended = jnp.dot(gating * context, w_out, precision=highest)
    d_context = (jnp.dot(cotangent, w_out.T, precision=highest) * gating).reshape(TOKENS, HEADS, head_dim)
    row_delta_all = lax.optimization_barrier(jnp.sum(d_context * context.reshape(TOKENS, HEADS, head_dim), axis=-1))

    def backward_block(index):
        soft_weights, pair_rows = weights_of(index)
        start = (index * TR).astype(jnp.int32)
        d_rows = lax.dynamic_slice_in_dim(d_context, start, TR, 0)
        row_delta = lax.dynamic_slice_in_dim(row_delta_all, start, TR, 0)
        d_probs = jnp.einsum('ihd,jhd->ihj', d_rows, values, precision=highest)
        d_scores = soft_weights * (d_probs - row_delta[:, :, None])
        _, pull = jax.vjp(bias_of, pair_rows, w_bias)
        return pull(d_scores)
    pair_parts, weight_parts = lax.map(backward_block, blocks)
    pair_grad = pair_parts.reshape(TOKENS, TOKENS, PAIR_C)
    bias_grad = lax.optimization_barrier(jnp.sum(weight_parts, axis=0))
    return (attended, pair_grad, bias_grad)
```

```python
import functools

import jax
import jax.numpy as jnp
from jax import lax
from jax.experimental import pallas as pl
from jax.experimental.pallas import tpu as pltpu
from jax.sharding import PartitionSpec as P

MESH = pl.DeviceIdType.MESH
VMEM_LIMIT = 56 * 1024 * 1024
CHUNK = 8
F32 = jnp.float32
BF16 = jnp.bfloat16
NN = (((1,), (0,)), ((), ()))
NT = (((1,), (1,)), ((), ()))


def split(x):
    hi = x.astype(BF16)
    return hi, (x - hi.astype(F32)).astype(BF16)


def stacked(x):
    return jnp.concatenate(split(x), axis=0)


def dot(a, b, dims):
    return lax.dot_general(a, b, dims, preferred_element_type=F32)


def dot3(both, b_hi, b_lo, dims):
    m = both.shape[0] // 2
    high = dot(both, b_hi, dims)
    return high[:m] + high[m:] + dot(both[:m], b_lo, dims)


def unit(x, width):
    centre = jnp.sum(x, axis=-1, keepdims=True) * (1.0 / width)
    x = x - centre
    spread = jnp.sum(x * x, axis=-1, keepdims=True) * (1.0 / width)
    scale = lax.rsqrt(spread + 1e-05)
    return x * scale, scale


def remote(src, dst, send_sem, recv_sem, **device):
    return pltpu.make_async_remote_copy(
        src_ref=src, dst_ref=dst, send_sem=send_sem, recv_sem=recv_sem,
        device_id=device, device_id_type=MESH,
    )


def greet(devices):
    barrier = pltpu.get_barrier_semaphore()
    for device in devices:
        pl.semaphore_signal(barrier, inc=1, device_id=device, device_id_type=MESH)
    pl.semaphore_wait(barrier, len(devices))


def scores_kernel(
    n_row, n_col, heads,
    single_ref, pair_hbm, gain_ref, pgain_ref, wq_hbm, wk_hbm, wv_hbm, wg_hbm, wbt_ref, wout_ref,
    cot_ref,
    att_ref, ds_ref,
    pair_v, wq_v, wk_v, wv_v, wg_v,
    tok, keyb, part_out, part_in, back, s_ref, dp_ref, q_ref, dc_ref, gate_b,
    kb_hi, kb_lo, vb_hi, vb_lo, stat, ctx_ref, ctx_out, ctx_in, gctx,
    w_sem, p_sem, send_sem, recv_sem, tree_send, tree_recv, mate_send, mate_recv,
):
    r = lax.axis_index("row")
    c = lax.axis_index("col")
    tq, blk = single_ref.shape
    width = blk * n_col
    dim = width // heads
    n_chunk = tq // CHUNK
    n_chip = n_row // 2
    bits = n_chip.bit_length() - 1
    parity = r % 2
    chip = r // 2

    weights = [(wq_hbm, wq_v), (wg_hbm, wg_v), (wk_hbm, wk_v), (wv_hbm, wv_v)]
    pair_copies = [
        pltpu.make_async_copy(
            pair_hbm.at[pl.ds(CHUNK * k, CHUNK)], pair_v.at[pl.ds(CHUNK * k, CHUNK)], p_sem.at[k]
        )
        for k in range(n_chunk)
    ]
    weight_copies = [
        pltpu.make_async_copy(src, dst, w_sem.at[k]) for k, (src, dst) in enumerate(weights)
    ]
    for copy in pair_copies[:2] + weight_copies + pair_copies[2:]:
        copy.start()

    def peer(d):
        return (c + d) % n_col

    mate = r + 1 - 2 * parity
    chip_bits = [(chip // (1 << e)) % 2 for e in range(bits)]
    col_bits = [(c // (1 << e)) % 2 for e in range(bits)]
    away = [a + b - 2 * a * b for a, b in zip(chip_bits, col_bits)]
    beside = [r + (2 << e) * (1 - 2 * chip_bits[e]) for e in range(bits)]
    greet(
        [{"col": peer(d)} for d in range(1, n_col)]
        + [{"row": row} for row in beside]
        + [{"row": mate}]
    )

    def spread_out(stage, src_of, dst_of):
        copies = []
        for d in range(1, n_col):
            copy = remote(
                src_of(d), dst_of(d), send_sem.at[stage, d], recv_sem.at[stage, d], col=peer(d)
            )
            copy.start()
            copies.append(copy)
        return copies

    tok_copies = spread_out(0, lambda d: single_ref, lambda d: tok.at[c])
    tok[c] = single_ref[...]

    cot = stacked(cot_ref[...])

    def part(owner):
        rows = wout_ref[pl.ds(pl.multiple_of(owner * blk, 8), blk), :]
        return dot3(cot, *split(rows), NT)

    for d in range(1, n_col):
        part_out[d] = part(peer(d))
    back_copies = spread_out(1, lambda d: part_out.at[d], lambda d: part_in.at[d])
    part_out[0] = part(c)

    wb = stacked(wbt_ref[...] * pgain_ref[...])

    def pair_bias(k):
        pair_copies[k].wait()
        x = pair_v[pl.ds(CHUNK * k, CHUNK)]
        x, _ = unit(x, x.shape[-1])
        hi, lo = split(x.reshape(-1, x.shape[-1]))
        bias = dot(wb, hi, NT)
        bias = bias[:heads] + bias[heads:] + dot(wb[:heads], lo, NT)
        keys_here = s_ref.shape[2]
        for i in range(CHUNK):
            s_ref[CHUNK * k + i] = bias[:, i * keys_here : (i + 1) * keys_here]

    at_source = sum(away) == 0
    forwards = []
    for t in range(n_col):
        block = (c - t + n_col) % n_col
        if t:
            tok_copies[t - 1].wait_recv()

        @pl.when(at_source)
        def _():
            keyb[parity, block] = tok[block]

        @pl.when(jnp.logical_not(at_source))
        def _():
            remote(
                keyb.at[parity, block], keyb.at[parity, block], tree_send.at[0, t],
                tree_recv.at[t], row=mate,
            ).wait_recv()

        for e in reversed(range(bits)):
            copy = remote(
                keyb.at[parity, block], keyb.at[parity, block], tree_send.at[e, t],
                tree_recv.at[t], row=beside[e],
            )
            forwards.append((sum(away[: e + 1]) == 0, copy))
            pl.when(forwards[-1][0])(copy.start)
        copy = remote(
            keyb.at[parity, block], keyb.at[parity, block], mate_send.at[t], mate_recv.at[t],
            row=mate,
        )
        copy.start()
        forwards.append((None, copy))
        for k in range(t * n_chunk // n_col, (t + 1) * n_chunk // n_col):
            pair_bias(k)

    for copy in back_copies:
        copy.wait_recv()
    total = part_out[0]
    for d in range(1, n_col):
        total = total + part_in[d]
    back[c] = total
    back_copies2 = spread_out(2, lambda d: back.at[c], lambda d: back.at[c])

    def project(both, w_ref):
        step = 256
        out = None
        for lo in range(0, width, step):
            piece = dot3(both[:, lo : lo + step], *split(w_ref[lo : lo + step, :]), NN)
            out = piece if out is None else out + piece
        return out

    def joined(ref, *lead):
        return jnp.concatenate([ref[(*lead, b)] for b in range(n_col)], axis=1)

    rows = stacked(unit(joined(tok), width)[0] * gain_ref[...])
    weight_copies[0].wait()
    q_ref[...] = project(rows, wq_v) * dim ** (-0.5)
    weight_copies[1].wait()
    gate = jax.nn.sigmoid(project(rows, wg_v))
    for b in range(n_col):
        gate_b[b] = gate[:, b * blk : (b + 1) * blk]

    for _, copy in forwards[bits :: bits + 1]:
        copy.wait_recv()
    tokens = jnp.concatenate([joined(keyb, 0), joined(keyb, 1)], axis=0)
    rows = stacked(unit(tokens, width)[0] * gain_ref[...])
    weight_copies[2].wait()
    kb_hi[...], kb_lo[...] = split(project(rows, wk_v))
    weight_copies[3].wait()
    vb_hi[...], vb_lo[...] = split(project(rows, wv_v))

    for copy in back_copies2:
        copy.wait_recv()
    dc_ref[...] = joined(back) * gate

    head_of = lax.broadcasted_iota(jnp.int32, (heads, width), 0) * dim
    feature = lax.broadcasted_iota(jnp.int32, (heads, width), 1)
    mask = jnp.where((feature >= head_of) & (feature < head_of + dim), 1.0, 0.0)
    flat = CHUNK * heads

    def by_head(ref, k):
        x = ref[pl.ds(pl.multiple_of(CHUNK * k, CHUNK), CHUNK), :]
        return stacked((x[:, None, :] * mask[None]).reshape(flat, width))

    lane = lax.broadcasted_iota(jnp.int32, (flat, 128), 1)

    def forward(k, carry):
        here = pl.ds(CHUNK * k, CHUNK)
        s = s_ref[here].reshape(flat, -1)
        s = s + dot3(by_head(q_ref, k), kb_hi[...], kb_lo[...], NT)
        top = jnp.max(s, axis=-1, keepdims=True)
        expo = jnp.exp(s - top)
        dp = dot3(by_head(dc_ref, k), vb_hi[...], vb_lo[...], NT)
        sums = jnp.sum(expo, axis=-1, keepdims=True)
        delta = jnp.sum(expo * dp, axis=-1, keepdims=True)
        s_ref[here] = expo.reshape(CHUNK, heads, -1)
        dp_ref[here] = dp.reshape(CHUNK, heads, -1)
        packed = jnp.where(lane == 0, top, jnp.where(lane == 1, sums, delta))
        stat[c, k] = packed.T[:8]
        return carry

    lax.fori_loop(0, n_chunk, forward, 0)
    stat_copies = spread_out(3, lambda d: stat.at[c], lambda d: stat.at[c])
    for copy in stat_copies:
        copy.wait_recv()

    def backward(k, carry):
        here = pl.ds(CHUNK * k, CHUNK)
        every = [stat[b, k] for b in range(n_col)]
        top = functools.reduce(jnp.maximum, [x[0:1] for x in every])
        factors = [jnp.exp(x[0:1] - top) for x in every]
        sums = sum(f * x[1:2] for f, x in zip(factors, every))
        delta = sum(f * x[2:3] for f, x in zip(factors, every)) / sums
        mine = jnp.exp(stat[c, k][0:1] - top) / sums
        sub = lax.broadcasted_iota(jnp.int32, (128, flat), 0)
        columns = jnp.where(sub == 0, mine, delta).T
        probs = s_ref[here].reshape(flat, -1) * columns[:, 0:1]
        ds = probs * (dp_ref[here].reshape(flat, -1) - columns[:, 1:2])
        ds_ref[here] = ds.reshape(CHUNK, heads, -1)
        wide = dot3(stacked(probs), vb_hi[...], vb_lo[...], NN).reshape(CHUNK, heads, width)
        ctx_ref[pl.ds(pl.multiple_of(CHUNK * k, CHUNK), CHUNK), :] = jnp.sum(wide * mask[None], axis=1)
        return carry

    lax.fori_loop(0, n_chunk, backward, 0)
    ctx = ctx_ref[...]
    for b in range(n_col):
        ctx_out[b] = ctx[:, b * blk : (b + 1) * blk]
    ctx_copies = spread_out(4, lambda d: ctx_out.at[peer(d)], lambda d: ctx_in.at[d])
    total = ctx_out[c]
    for d, copy in enumerate(ctx_copies, 1):
        copy.wait_recv()
        total = total + ctx_in[d]
    gctx[c] = total * gate_b[c]
    gctx_copies = spread_out(5, lambda d: gctx.at[c], lambda d: gctx.at[c])
    for copy in gctx_copies:
        copy.wait_recv()
    out = None
    for b in range(n_col):
        piece = dot3(stacked(gctx[b]), *split(wout_ref[b * blk : (b + 1) * blk, :]), NN)
        out = piece if out is None else out + piece
    att_ref[...] = out

    for copy in tok_copies + back_copies + back_copies2 + stat_copies + ctx_copies + gctx_copies:
        copy.wait_send()
    for condition, copy in forwards:
        if condition is None:
            copy.wait_send()
        else:
            pl.when(condition)(copy.wait_send)


def pair_kernel(heads, pair_ref, ds_ref, pgain_ref, wbt_ref, grad_ref, weight_ref, wide_hi, wide_lo):
    channels = pair_ref.shape[2]
    keys = pair_ref.shape[1]

    @pl.when(pl.program_id(0) == 0)
    def _():
        hi, lo = split(wbt_ref[...] * pgain_ref[...])
        for ref, value in ((wide_hi, hi), (wide_lo, lo)):
            ref[...] = jnp.zeros_like(ref)
            for i in range(CHUNK):
                ref[heads * i : heads * (i + 1), channels * i : channels * (i + 1)] = value
        weight_ref[...] = jnp.zeros_like(weight_ref)

    x, scale = unit(pair_ref[...], channels)
    ds = ds_ref[...]
    across = jnp.concatenate([ds[i] for i in range(CHUNK)], axis=1)
    weight_ref[...] += dot3(stacked(across), *split(x.reshape(-1, channels)), NN)
    columns = ds.reshape(CHUNK * heads, keys).T
    d_unit = dot3(stacked(columns), wide_hi[...], wide_lo[...], NN)
    for i in range(CHUNK):
        d = d_unit[:, channels * i : channels * (i + 1)]
        centre = jnp.sum(d, axis=-1, keepdims=True) * (1.0 / channels)
        slope = jnp.sum(d * x[i], axis=-1, keepdims=True) * (1.0 / channels)
        grad_ref[i] = (d - centre - x[i] * slope) * scale[i]


def sum_kernel(n_row, n_col, part_ref, pgain_ref, out_ref, near, far, total, send_sem, recv_sem):
    r = lax.axis_index("row")
    c = lax.axis_index("col")
    greet(
        [{"row": (r + d) % n_row} for d in range(1, n_row)]
        + [{"col": (c + d) % n_col} for d in range(1, n_col)]
    )
    copies = []
    for d in range(1, n_row):
        copy = remote(
            part_ref, near.at[d], send_sem.at[d], recv_sem.at[d], row=(r + d) % n_row
        )
        copy.start()
        copies.append(copy)
    so_far = part_ref[...]
    for d, copy in enumerate(copies, 1):
        copy.wait_recv()
        so_far = so_far + near[d]
    total[...] = so_far
    later = []
    for d in range(1, n_col):
        k = n_row + d
        copy = remote(total, far.at[d], send_sem.at[k], recv_sem.at[k], col=(c + d) % n_col)
        copy.start()
        later.append(copy)
    for d, copy in enumerate(later, 1):
        copy.wait_recv()
        so_far = so_far + far[d]
    so_far = so_far * pgain_ref[...]
    heads, channels = so_far.shape
    square = jnp.concatenate([so_far, jnp.zeros((channels - heads, channels), F32)], axis=0)
    out_ref[...] = square.T[:, :heads]
    for copy in copies + later:
        copy.wait_send()


def local(
    n_row, n_col,
    single, pair, single_gain, pair_gain, w_query, w_key, w_value, w_gate, w_bias, w_out, cotangent
):
    tq, blk = single.shape
    width = single_gain.shape[0]
    channels, heads = w_bias.shape
    keys = pair.shape[1]
    n_chunk = tq // CHUNK
    vmem = pl.BlockSpec(memory_space=pltpu.VMEM)
    hbm = pl.BlockSpec(memory_space=pl.ANY)
    bits = (n_row // 2).bit_length() - 1
    w_bias_t = w_bias.T
    pair_gain = pair_gain.reshape(1, channels)
    single_gain = single_gain.reshape(1, width)
    blocks = pltpu.VMEM((n_col, tq, blk), F32)
    dma = pltpu.SemaphoreType.DMA
    attended, d_scores = pl.pallas_call(
        functools.partial(scores_kernel, n_row, n_col, heads),
        out_shape=(
            jax.ShapeDtypeStruct((tq, blk), F32),
            jax.ShapeDtypeStruct((tq, heads, keys), F32),
        ),
        in_specs=[vmem, hbm, vmem, vmem, hbm, hbm, hbm, hbm, vmem, vmem, vmem],
        out_specs=(vmem, vmem),
        scratch_shapes=[
            pltpu.VMEM(pair.shape, F32),
            *[pltpu.VMEM((width, width), F32)] * 4,
            blocks,
            pltpu.VMEM((2, n_col, tq, blk), F32),
            blocks, blocks, blocks,
            pltpu.VMEM((tq, heads, keys), F32),
            pltpu.VMEM((tq, heads, keys), F32),
            pltpu.VMEM((tq, width), F32),
            pltpu.VMEM((tq, width), F32),
            blocks,
            *[pltpu.VMEM((keys, width), BF16)] * 4,
            pltpu.VMEM((n_col, n_chunk, 8, CHUNK * heads), F32),
            pltpu.VMEM((tq, width), F32),
            blocks, blocks, blocks,
            dma((4,)), dma((n_chunk,)), dma((6, n_col)), dma((6, n_col)),
            dma((bits, n_col)), dma((n_col,)), dma((n_col,)), dma((n_col,)),
        ],
        compiler_params=pltpu.CompilerParams(
            collective_id=0, has_side_effects=True, vmem_limit_bytes=VMEM_LIMIT
        ),
        name="attend",
    )(
        single, pair, single_gain, pair_gain, w_query, w_key, w_value, w_gate, w_bias_t, w_out,
        cotangent,
    )
    whole = lambda shape: pl.BlockSpec(shape, lambda k: (0,) * len(shape))
    pair_grad, weight_part = pl.pallas_call(
        functools.partial(pair_kernel, heads),
        grid=(n_chunk,),
        out_shape=(
            jax.ShapeDtypeStruct(pair.shape, F32),
            jax.ShapeDtypeStruct((heads, channels), F32),
        ),
        in_specs=[
            pl.BlockSpec((CHUNK, keys, channels), lambda k: (k, 0, 0)),
            pl.BlockSpec((CHUNK, heads, keys), lambda k: (k, 0, 0)),
            whole((1, channels)),
            whole((heads, channels)),
        ],
        out_specs=(
            pl.BlockSpec((CHUNK, keys, channels), lambda k: (k, 0, 0)),
            whole((heads, channels)),
        ),
        scratch_shapes=[pltpu.VMEM((CHUNK * heads, CHUNK * channels), BF16)] * 2,
        compiler_params=pltpu.CompilerParams(vmem_limit_bytes=VMEM_LIMIT),
        name="pair_back",
    )(pair, d_scores, pair_gain, w_bias_t)
    bias_grad = pl.pallas_call(
        functools.partial(sum_kernel, n_row, n_col),
        out_shape=jax.ShapeDtypeStruct((channels, heads), F32),
        in_specs=[vmem, vmem],
        out_specs=vmem,
        scratch_shapes=[
            pltpu.VMEM((n_row, heads, channels), F32),
            pltpu.VMEM((n_col, heads, channels), F32),
            pltpu.VMEM((heads, channels), F32),
            dma((n_row + n_col,)), dma((n_row + n_col,)),
        ],
        compiler_params=pltpu.CompilerParams(collective_id=1, has_side_effects=True),
        name="sum_bias",
    )(weight_part, pair_gain)
    return (attended, pair_grad, bias_grad)


def solution(mesh):
    placed = (
        P("row", "col"),
        P("row", "col", None),
        P(),
        P(),
        P(),
        P(),
        P(),
        P(),
        P(),
        P(None, "col"),
        P("row", "col"),
    )
    return jax.shard_map(
        functools.partial(local, mesh.shape["row"], mesh.shape["col"]),
        mesh=mesh,
        in_specs=placed,
        out_specs=(P("row", "col"), P("row", "col", None), P()),
        check_vma=False,
    )
```

```python
import functools

import jax
import jax.numpy as jnp
from jax import lax
from jax.experimental import pallas as pl
from jax.experimental.pallas import tpu as pltpu
from jax.sharding import PartitionSpec as P

MESH = pl.DeviceIdType.MESH
VMEM_LIMIT = 56 * 1024 * 1024
CHUNK = 8
F32 = jnp.float32
BF16 = jnp.bfloat16
NN = (((1,), (0,)), ((), ()))
NT = (((1,), (1,)), ((), ()))


def split(x):
    hi = x.astype(BF16)
    return hi, (x - hi.astype(F32)).astype(BF16)


def stacked(x):
    return jnp.concatenate(split(x), axis=0)


def dot(a, b, dims):
    return lax.dot_general(a, b, dims, preferred_element_type=F32)


def dot3(both, b_hi, b_lo, dims):
    m = both.shape[0] // 2
    high = dot(both, b_hi, dims)
    return high[:m] + high[m:] + dot(both[:m], b_lo, dims)


def dot_rows(both, b_both):
    m, n = both.shape[0] // 2, b_both.shape[0] // 2
    out = dot(both, b_both, NT)
    return out[:m, :n] + (out[:m, n:] + out[m:, :n])


def dot_deep(x, b_both, b_hi):
    hi, lo = split(x)
    return dot(jnp.concatenate([hi, hi], axis=1), b_both, NN) + dot(lo, b_hi, NN)


def unit(x, width):
    centre = jnp.sum(x, axis=-1, keepdims=True) * (1.0 / width)
    x = x - centre
    spread = jnp.sum(x * x, axis=-1, keepdims=True) * (1.0 / width)
    scale = lax.rsqrt(spread + 1e-05)
    return x * scale, scale


def remote(src, dst, send_sem, recv_sem, **device):
    return pltpu.make_async_remote_copy(
        src_ref=src, dst_ref=dst, send_sem=send_sem, recv_sem=recv_sem,
        device_id=device, device_id_type=MESH,
    )


def greet(devices):
    barrier = pltpu.get_barrier_semaphore()
    for device in devices:
        pl.semaphore_signal(barrier, inc=1, device_id=device, device_id_type=MESH)
    pl.semaphore_wait(barrier, len(devices))


def layer_kernel(
    n_row, n_col, heads,
    single_ref, pair_hbm, gain_ref, pgain_ref, wq_hbm, wk_hbm, wv_hbm, wg_hbm, wbt_ref, wout_ref,
    cot_ref,
    att_ref, grad_hbm, bgrad_ref,
    pair_v, scale_v, wq_v, wk_v, wv_v, wg_v,
    tok, keyb, part_out, part_in, back, s_ref, dp_ref, q_ref, dc_ref, gate_b,
    kb, vb, stat, ctx_ref, ctx_out, ctx_in, gctx,
    w_hi, w_lo, wide_b, total_w, near, far,
    sum_send, sum_recv, o_sem, w_sem, p_sem, send_sem, recv_sem, tree_send, tree_recv, mate_send, mate_recv,
):
    r = lax.axis_index("row")
    c = lax.axis_index("col")
    tq, blk = single_ref.shape
    width = blk * n_col
    dim = width // heads
    n_chunk = tq // CHUNK
    n_chip = n_row // 2
    bits = n_chip.bit_length() - 1
    parity = r % 2
    chip = r // 2

    weights = [(wq_hbm, wq_v), (wg_hbm, wg_v), (wk_hbm, wk_v), (wv_hbm, wv_v)]
    pair_copies = [
        pltpu.make_async_copy(
            pair_hbm.at[pl.ds(CHUNK * k, CHUNK)], pair_v.at[pl.ds(CHUNK * k, CHUNK)], p_sem.at[k]
        )
        for k in range(n_chunk)
    ]
    weight_copies = [
        pltpu.make_async_copy(src, dst, w_sem.at[k]) for k, (src, dst) in enumerate(weights)
    ]
    for copy in pair_copies[:2] + weight_copies + pair_copies[2:]:
        copy.start()

    def peer(d):
        return (c + d) % n_col

    mate = r + 1 - 2 * parity
    chip_bits = [(chip // (1 << e)) % 2 for e in range(bits)]
    col_bits = [(c // (1 << e)) % 2 for e in range(bits)]
    away = [a + b - 2 * a * b for a, b in zip(chip_bits, col_bits)]
    beside = [r + (2 << e) * (1 - 2 * chip_bits[e]) for e in range(bits)]
    greet(
        [{"col": peer(d)} for d in range(1, n_col)]
        + [{"row": (r + d) % n_row} for d in range(1, n_row)]
    )

    def spread_out(stage, src_of, dst_of):
        copies = []
        for d in range(1, n_col):
            copy = remote(
                src_of(d), dst_of(d), send_sem.at[stage, d], recv_sem.at[stage, d], col=peer(d)
            )
            copy.start()
            copies.append(copy)
        return copies

    tok_copies = spread_out(0, lambda d: single_ref, lambda d: tok.at[c])
    tok[c] = single_ref[...]

    part = dot3(stacked(cot_ref[...]), *split(wout_ref[...]), NN)
    for b in range(n_col):
        part_out[b] = part[:, b * blk : (b + 1) * blk]
    back_copies = spread_out(1, lambda d: part_out.at[peer(d)], lambda d: part_in.at[d])
    gain = gain_ref[...].reshape(1, width)

    weight_t = wbt_ref[...] * pgain_ref[...]
    wb = stacked(weight_t)
    wb = jnp.concatenate([wb, jnp.concatenate([wb[:heads], jnp.zeros_like(wb[:heads])], 0)], 1)

    def pair_bias(k):
        pair_copies[k].wait()
        x = pair_v[pl.ds(CHUNK * k, CHUNK)]
        x, scale = unit(x, x.shape[-1])
        pair_v[pl.ds(CHUNK * k, CHUNK)] = x
        scale_v[pl.ds(CHUNK * k, CHUNK)] = jnp.broadcast_to(scale, x.shape)
        bias = dot(wb, jnp.concatenate(split(x.reshape(-1, x.shape[-1])), axis=1), NT)
        bias = bias[:heads] + bias[heads:]
        keys_here = s_ref.shape[2]
        for i in range(CHUNK):
            s_ref[CHUNK * k + i] = bias[:, i * keys_here : (i + 1) * keys_here]

    at_source = sum(away) == 0
    forwards = []
    for t in range(n_col):
        block = (c - t + n_col) % n_col
        if t:
            tok_copies[t - 1].wait_recv()

        @pl.when(at_source)
        def _():
            keyb[parity, block] = tok[block]

        @pl.when(jnp.logical_not(at_source))
        def _():
            remote(
                keyb.at[parity, block], keyb.at[parity, block], tree_send.at[0, t],
                tree_recv.at[t], row=mate,
            ).wait_recv()

        for e in reversed(range(bits)):
            copy = remote(
                keyb.at[parity, block], keyb.at[parity, block], tree_send.at[e, t],
                tree_recv.at[t], row=beside[e],
            )
            forwards.append((sum(away[: e + 1]) == 0, copy))
            pl.when(forwards[-1][0])(copy.start)
        copy = remote(
            keyb.at[parity, block], keyb.at[parity, block], mate_send.at[t], mate_recv.at[t],
            row=mate,
        )
        copy.start()
        forwards.append((None, copy))
        if t < n_col - 1:
            early = n_chunk - 3
            for k in range(t * early // (n_col - 1), (t + 1) * early // (n_col - 1)):
                pair_bias(k)

    for copy in back_copies:
        copy.wait_recv()
    total = part_out[c]
    for d in range(1, n_col):
        total = total + part_in[d]
    back[c] = total
    back_copies2 = spread_out(2, lambda d: back.at[c], lambda d: back.at[c])

    for k in range(n_chunk - 3, n_chunk):
        pair_bias(k)
    step = 256
    for k, (_, w_ref) in enumerate(weights):
        weight_copies[k].wait()
        for lo in range(0, width, step):
            w_hi[k, lo : lo + step], w_lo[k, lo : lo + step] = split(w_ref[lo : lo + step, :])
    wide_b[...] = jnp.zeros_like(wide_b)
    centred = weight_t - jnp.sum(weight_t, axis=1, keepdims=True) * (1.0 / weight_t.shape[1])
    channels = weight_t.shape[1]
    for half, value in enumerate(split(centred)):
        for i in range(CHUNK):
            row = half * CHUNK * heads + heads * i
            wide_b[row : row + heads, channels * i : channels * (i + 1)] = value

    def project(both, k):
        out = None
        for lo in range(0, width, step):
            piece = dot3(
                both[:, lo : lo + step], w_hi[k, lo : lo + step], w_lo[k, lo : lo + step], NN
            )
            out = piece if out is None else out + piece
        return out

    def joined(ref, *lead):
        return jnp.concatenate([ref[(*lead, b)] for b in range(n_col)], axis=1)

    rows = stacked(unit(joined(tok), width)[0] * gain)
    q_ref[...] = project(rows, 0) * dim ** (-0.5)
    gate = jax.nn.sigmoid(project(rows, 1))
    for b in range(n_col):
        gate_b[b] = gate[:, b * blk : (b + 1) * blk]

    for _, copy in forwards[bits :: bits + 1]:
        copy.wait_recv()
    tokens = jnp.concatenate([joined(keyb, 0), joined(keyb, 1)], axis=0)
    rows = stacked(unit(tokens, width)[0] * gain)
    kb[...] = stacked(project(rows, 2))
    vb[...] = stacked(project(rows, 3))

    for copy in back_copies2:
        copy.wait_recv()
    dc_ref[...] = joined(back) * gate

    head_of = lax.broadcasted_iota(jnp.int32, (heads, width), 0) * dim
    feature = lax.broadcasted_iota(jnp.int32, (heads, width), 1)
    mask = jnp.where((feature >= head_of) & (feature < head_of + dim), 1.0, 0.0)
    flat = CHUNK * heads

    def by_head(ref, k):
        x = ref[pl.ds(pl.multiple_of(CHUNK * k, CHUNK), CHUNK), :]
        return stacked((x[:, None, :] * mask[None]).reshape(flat, width))

    lane = lax.broadcasted_iota(jnp.int32, (flat, 128), 1)

    def forward(k, carry):
        here = pl.ds(CHUNK * k, CHUNK)
        s = s_ref[here].reshape(flat, -1)
        s = s + dot_rows(by_head(q_ref, k), kb[...])
        top = jnp.max(s, axis=-1, keepdims=True)
        expo = jnp.exp(s - top)
        dp = dot_rows(by_head(dc_ref, k), vb[...])
        sums = jnp.sum(expo, axis=-1, keepdims=True)
        delta = jnp.sum(expo * dp, axis=-1, keepdims=True)
        s_ref[here] = expo.reshape(CHUNK, heads, -1)
        dp_ref[here] = dp.reshape(CHUNK, heads, -1)
        packed = jnp.where(lane == 0, top, jnp.where(lane == 1, sums, delta))
        stat[c, k] = packed.T[:8]
        return carry

    lax.fori_loop(0, n_chunk, forward, 0)
    stat_copies = spread_out(3, lambda d: stat.at[c], lambda d: stat.at[c])
    for copy in stat_copies:
        copy.wait_recv()

    def backward(k, carry):
        here = pl.ds(CHUNK * k, CHUNK)
        every = [stat[b, k] for b in range(n_col)]
        top = functools.reduce(jnp.maximum, [x[0:1] for x in every])
        factors = [jnp.exp(x[0:1] - top) for x in every]
        sums = sum(f * x[1:2] for f, x in zip(factors, every))
        delta = sum(f * x[2:3] for f, x in zip(factors, every)) / sums
        mine = jnp.exp(stat[c, k][0:1] - top) / sums
        sub = lax.broadcasted_iota(jnp.int32, (128, flat), 0)
        columns = jnp.where(sub == 0, mine, delta).T
        probs = s_ref[here].reshape(flat, -1) * columns[:, 0:1]
        ds = probs * (dp_ref[here].reshape(flat, -1) - columns[:, 1:2])
        ds = ds.reshape(CHUNK, heads, -1)
        dp_ref[here] = ds
        across = jnp.concatenate([ds[i] for i in range(CHUNK)], axis=1)
        x_hi, x_lo = split(pair_v[here].reshape(-1, channels))
        both = dot(stacked(across), jnp.concatenate([x_hi, x_lo], axis=1), NN)
        carry = carry + (
            both[:heads, :channels] + (both[:heads, channels:] + both[heads:, :channels])
        )
        keys_here = vb.shape[0] // 2
        wide = dot_deep(probs, vb[...], vb[:keys_here]).reshape(CHUNK, heads, width)
        ctx_ref[pl.ds(pl.multiple_of(CHUNK * k, CHUNK), CHUNK), :] = jnp.sum(wide * mask[None], axis=1)
        return carry

    total_w[0] = lax.fori_loop(0, n_chunk, backward, jnp.zeros((heads, channels), F32))
    near_copies = []
    for d in range(1, n_row):
        copy = remote(
            total_w.at[0], near.at[d], sum_send.at[d], sum_recv.at[d], row=(r + d) % n_row
        )
        copy.start()
        near_copies.append(copy)
    ctx = ctx_ref[...]
    for b in range(n_col):
        ctx_out[b] = ctx[:, b * blk : (b + 1) * blk]
    ctx_copies = spread_out(4, lambda d: ctx_out.at[peer(d)], lambda d: ctx_in.at[d])

    def out_copy(k):
        here = pl.ds(CHUNK * k, CHUNK)
        return pltpu.make_async_copy(pair_v.at[here], grad_hbm.at[here], o_sem.at[k])

    def pair_back(k, carry):
        ds = dp_ref[pl.ds(CHUNK * k, CHUNK)]
        columns = ds.reshape(flat, -1).T
        d_unit = dot_deep(columns, wide_b[...], wide_b[:flat])
        for i in range(CHUNK):
            d = d_unit[:, channels * i : channels * (i + 1)]
            x = pair_v[CHUNK * k + i]
            slope = jnp.sum(d * x, axis=-1, keepdims=True) * (1.0 / channels)
            pair_v[CHUNK * k + i] = (d - x * slope) * scale_v[CHUNK * k + i]
        out_copy(k).start()
        return carry

    lax.fori_loop(0, n_chunk // 2, pair_back, 0)

    total = total_w[0]
    for d, copy in enumerate(near_copies, 1):
        copy.wait_recv()
        total = total + near[d]
    total_w[1] = total
    far_copies = []
    for d in range(1, n_col):
        k = n_row + d
        copy = remote(total_w.at[1], far.at[d], sum_send.at[k], sum_recv.at[k], col=peer(d))
        copy.start()
        far_copies.append(copy)
    total = ctx_out[c]
    for d, copy in enumerate(ctx_copies, 1):
        copy.wait_recv()
        total = total + ctx_in[d]
    gctx[c] = total * gate_b[c]
    gctx_copies = spread_out(5, lambda d: gctx.at[c], lambda d: gctx.at[c])

    lax.fori_loop(n_chunk // 2, n_chunk, pair_back, 0)

    total = total_w[1]
    for d, copy in enumerate(far_copies, 1):
        copy.wait_recv()
        total = total + far[d]
    bgrad_ref[...] = total * pgain_ref[...]
    for copy in gctx_copies:
        copy.wait_recv()
    att_ref[...] = dot3(stacked(joined(gctx)), *split(wout_ref[...]), NT)

    waits = tok_copies + back_copies + back_copies2 + stat_copies + ctx_copies + gctx_copies
    for copy in waits + near_copies + far_copies:
        copy.wait_send()
    for condition, copy in forwards:
        if condition is None:
            copy.wait_send()
        else:
            pl.when(condition)(copy.wait_send)
    for k in range(n_chunk):
        out_copy(k).wait()


def local(
    n_row, n_col,
    single, pair, single_gain, pair_gain, w_query, w_key, w_value, w_gate, w_bias, w_out, cotangent
):
    tq, blk = single.shape
    width = single_gain.shape[0]
    channels, heads = w_bias.shape
    keys = pair.shape[1]
    n_chunk = tq // CHUNK
    vmem = pl.BlockSpec(memory_space=pltpu.VMEM)
    hbm = pl.BlockSpec(memory_space=pl.ANY)
    bits = (n_row // 2).bit_length() - 1
    w_bias_t = w_bias.T
    pair_gain = pair_gain.reshape(1, channels)
    blocks = pltpu.VMEM((n_col, tq, blk), F32)
    dma = pltpu.SemaphoreType.DMA
    attended, pair_grad, bias_grad = pl.pallas_call(
        functools.partial(layer_kernel, n_row, n_col, heads),
        out_shape=(
            jax.ShapeDtypeStruct((tq, blk), F32),
            jax.ShapeDtypeStruct(pair.shape, F32),
            jax.ShapeDtypeStruct((heads, channels), F32),
        ),
        in_specs=[vmem, hbm, vmem, vmem, hbm, hbm, hbm, hbm, vmem, vmem, vmem],
        out_specs=(vmem, hbm, vmem),
        scratch_shapes=[
            pltpu.VMEM(pair.shape, F32),
            pltpu.VMEM(pair.shape, F32),
            *[pltpu.VMEM((width, width), F32)] * 4,
            blocks,
            pltpu.VMEM((2, n_col, tq, blk), F32),
            blocks, blocks, blocks,
            pltpu.VMEM((tq, heads, keys), F32),
            pltpu.VMEM((tq, heads, keys), F32),
            pltpu.VMEM((tq, width), F32),
            pltpu.VMEM((tq, width), F32),
            blocks,
            *[pltpu.VMEM((2 * keys, width), BF16)] * 2,
            pltpu.VMEM((n_col, n_chunk, 8, CHUNK * heads), F32),
            pltpu.VMEM((tq, width), F32),
            blocks, blocks, blocks,
            *[pltpu.VMEM((4, width, width), BF16)] * 2,
            pltpu.VMEM((2 * CHUNK * heads, CHUNK * channels), BF16),
            pltpu.VMEM((2, heads, channels), F32),
            pltpu.VMEM((n_row, heads, channels), F32),
            pltpu.VMEM((n_col, heads, channels), F32),
            dma((n_row + n_col,)), dma((n_row + n_col,)), dma((n_chunk,)),
            dma((4,)), dma((n_chunk,)), dma((6, n_col)), dma((6, n_col)),
            dma((bits, n_col)), dma((n_col,)), dma((n_col,)), dma((n_col,)),
        ],
        compiler_params=pltpu.CompilerParams(
            collective_id=0, has_side_effects=True, vmem_limit_bytes=VMEM_LIMIT
        ),
        name="layer",
    )(
        single, pair, single_gain, pair_gain, w_query, w_key, w_value, w_gate, w_bias_t, w_out.T,
        cotangent,
    )
    return (attended, pair_grad, bias_grad.T)


def solution(mesh):
    placed = (
        P("row", "col"),
        P("row", "col", None),
        P(),
        P(),
        P(),
        P(),
        P(),
        P(),
        P(),
        P(None, "col"),
        P("row", "col"),
    )
    return jax.shard_map(
        functools.partial(local, mesh.shape["row"], mesh.shape["col"]),
        mesh=mesh,
        in_specs=placed,
        out_specs=(P("row", "col"), P("row", "col", None), P()),
        check_vma=False,
    )
```

```python
import functools

import jax
import jax.numpy as jnp
from jax import lax
from jax.experimental import pallas as pl
from jax.experimental.pallas import tpu as pltpu
from jax.sharding import PartitionSpec as P

MESH = pl.DeviceIdType.MESH
VMEM_LIMIT = 48 * 1024 * 1024
CHUNK = 8
F32 = jnp.float32
BF16 = jnp.bfloat16
NN = (((1,), (0,)), ((), ()))
NT = (((1,), (1,)), ((), ()))


def split(x):
    hi = x.astype(BF16)
    return hi, (x - hi.astype(F32)).astype(BF16)


def stacked(x):
    return jnp.concatenate(split(x), axis=0)


def dot(a, b, dims):
    return lax.dot_general(a, b, dims, preferred_element_type=F32)


def dot3(both, b_hi, b_lo, dims):
    m = both.shape[0] // 2
    high = dot(both, b_hi, dims)
    return high[:m] + high[m:] + dot(both[:m], b_lo, dims)


def dot_rows(both, b_both):
    m, n = both.shape[0] // 2, b_both.shape[0] // 2
    out = dot(both, b_both, NT)
    return out[:m, :n] + (out[:m, n:] + out[m:, :n])


def dot_deep(x, b_both, b_hi):
    hi, lo = split(x)
    return dot(jnp.concatenate([hi, hi], axis=1), b_both, NN) + dot(lo, b_hi, NN)


def unit(x, width):
    centre = jnp.sum(x, axis=-1, keepdims=True) * (1.0 / width)
    x = x - centre
    spread = jnp.sum(x * x, axis=-1, keepdims=True) * (1.0 / width)
    scale = lax.rsqrt(spread + 1e-05)
    return x * scale, scale


def remote(src, dst, send_sem, recv_sem, **device):
    return pltpu.make_async_remote_copy(
        src_ref=src, dst_ref=dst, send_sem=send_sem, recv_sem=recv_sem,
        device_id=device, device_id_type=MESH,
    )


def greet(devices):
    barrier = pltpu.get_barrier_semaphore()
    for device in devices:
        pl.semaphore_signal(barrier, inc=1, device_id=device, device_id_type=MESH)
    pl.semaphore_wait(barrier, len(devices))


def layer_kernel(
    n_row, n_col, heads,
    single_ref, pair_hbm, gain_ref, pgain_ref, wq_hbm, wk_hbm, wv_hbm, wg_hbm, wbt_ref, wout_ref,
    cot_ref,
    att_ref, grad_ref, bgrad_ref,
    pair_v, scale_v, wq_v, wk_v, wv_v, wg_v,
    tok, keyb, part_out, part_in, back, s_ref, dp_ref, q_ref, dc_ref, gate_b,
    kb, vb, stat, ctx_ref, ctx_out, ctx_in, gctx,
    w_hi, w_lo, wide_b, total_w, near, far, factor,
    sum_send, sum_recv, w_sem, p_sem, send_sem, recv_sem, tree_send, tree_recv, mate_send, mate_recv,
):
    r = lax.axis_index("row")
    c = lax.axis_index("col")
    tq, blk = single_ref.shape
    width = blk * n_col
    dim = width // heads
    n_chunk = tq // CHUNK
    n_chip = n_row // 2
    bits = n_chip.bit_length() - 1
    parity = r % 2
    chip = r // 2

    weights = [(wq_hbm, wq_v), (wg_hbm, wg_v), (wk_hbm, wk_v), (wv_hbm, wv_v)]
    pair_copies = [
        pltpu.make_async_copy(
            pair_hbm.at[pl.ds(CHUNK * k, CHUNK)], pair_v.at[pl.ds(CHUNK * k, CHUNK)], p_sem.at[k]
        )
        for k in range(n_chunk)
    ]
    weight_copies = [
        pltpu.make_async_copy(src, dst, w_sem.at[k]) for k, (src, dst) in enumerate(weights)
    ]
    for copy in pair_copies[:2] + weight_copies + pair_copies[2:]:
        copy.start()

    def peer(d):
        return (c + d) % n_col

    mate = r + 1 - 2 * parity
    chip_bits = [(chip // (1 << e)) % 2 for e in range(bits)]
    col_bits = [(c // (1 << e)) % 2 for e in range(bits)]
    away = [a + b - 2 * a * b for a, b in zip(chip_bits, col_bits)]
    beside = [r + (2 << e) * (1 - 2 * chip_bits[e]) for e in range(bits)]
    greet(
        [{"col": peer(d)} for d in range(1, n_col)]
        + [{"row": (r + d) % n_row} for d in range(1, n_row)]
    )

    def spread_out(stage, src_of, dst_of):
        copies = []
        for d in range(1, n_col):
            copy = remote(
                src_of(d), dst_of(d), send_sem.at[stage, d], recv_sem.at[stage, d], col=peer(d)
            )
            copy.start()
            copies.append(copy)
        return copies

    tok_copies = spread_out(0, lambda d: single_ref, lambda d: tok.at[c])
    tok[c] = single_ref[...]

    part = dot3(stacked(cot_ref[...]), *split(wout_ref[...]), NN)
    for b in range(n_col):
        part_out[b] = part[:, b * blk : (b + 1) * blk]
    gain = gain_ref[...].reshape(1, width)

    weight_t = wbt_ref[...] * pgain_ref[...]
    wb = stacked(weight_t)
    wb = jnp.concatenate([wb, jnp.concatenate([wb[:heads], jnp.zeros_like(wb[:heads])], 0)], 1)

    def pair_bias(k):
        pair_copies[k].wait()
        x = pair_v[pl.ds(CHUNK * k, CHUNK)]
        x, scale = unit(x, x.shape[-1])
        pair_v[pl.ds(CHUNK * k, CHUNK)] = x
        scale_v[pl.ds(CHUNK * k, CHUNK)] = jnp.broadcast_to(scale, x.shape)
        bias = dot(wb, jnp.concatenate(split(x.reshape(-1, x.shape[-1])), axis=1), NT)
        bias = bias[:heads] + bias[heads:]
        keys_here = s_ref.shape[2]
        for i in range(CHUNK):
            s_ref[CHUNK * k + i] = bias[:, i * keys_here : (i + 1) * keys_here]

    at_source = sum(away) == 0
    forwards = []
    for t in range(n_col):
        block = (c - t + n_col) % n_col
        if t:
            tok_copies[t - 1].wait_recv()

        @pl.when(at_source)
        def _():
            keyb[parity, block] = tok[block]

        @pl.when(jnp.logical_not(at_source))
        def _():
            remote(
                keyb.at[parity, block], keyb.at[parity, block], tree_send.at[0, t],
                tree_recv.at[t], row=mate,
            ).wait_recv()

        for e in reversed(range(bits)):
            copy = remote(
                keyb.at[parity, block], keyb.at[parity, block], tree_send.at[e, t],
                tree_recv.at[t], row=beside[e],
            )
            forwards.append((sum(away[: e + 1]) == 0, copy))
            pl.when(forwards[-1][0])(copy.start)
        copy = remote(
            keyb.at[parity, block], keyb.at[parity, block], mate_send.at[t], mate_recv.at[t],
            row=mate,
        )
        copy.start()
        forwards.append((None, copy))
        if t == n_col - 2:
            back_copies = spread_out(1, lambda d: part_out.at[peer(d)], lambda d: part_in.at[d])
        if t < n_col - 1:
            early = n_chunk - 3
            for k in range(t * early // (n_col - 1), (t + 1) * early // (n_col - 1)):
                pair_bias(k)

    for copy in back_copies:
        copy.wait_recv()
    total = part_out[c]
    for d in range(1, n_col):
        total = total + part_in[d]
    back[c] = total
    back_copies2 = spread_out(2, lambda d: back.at[c], lambda d: back.at[c])

    for k in range(n_chunk - 3, n_chunk):
        pair_bias(k)
    step = 256
    for k, (_, w_ref) in enumerate(weights):
        weight_copies[k].wait()
        for lo in range(0, width, step):
            w_hi[k, lo : lo + step], w_lo[k, lo : lo + step] = split(w_ref[lo : lo + step, :])
    wide_b[...] = jnp.zeros_like(wide_b)
    centred = weight_t - jnp.sum(weight_t, axis=1, keepdims=True) * (1.0 / weight_t.shape[1])
    channels = weight_t.shape[1]
    for half, value in enumerate(split(centred)):
        for i in range(CHUNK):
            row = half * CHUNK * heads + heads * i
            wide_b[row : row + heads, channels * i : channels * (i + 1)] = value

    def project(both, k):
        out = None
        for lo in range(0, width, step):
            piece = dot3(
                both[:, lo : lo + step], w_hi[k, lo : lo + step], w_lo[k, lo : lo + step], NN
            )
            out = piece if out is None else out + piece
        return out

    def joined(ref, *lead):
        return jnp.concatenate([ref[(*lead, b)] for b in range(n_col)], axis=1)

    rows = stacked(unit(joined(tok), width)[0] * gain)
    q_ref[...] = project(rows, 0) * dim ** (-0.5)
    gate = jax.nn.sigmoid(project(rows, 1))
    for b in range(n_col):
        gate_b[b] = gate[:, b * blk : (b + 1) * blk]

    for _, copy in forwards[bits :: bits + 1]:
        copy.wait_recv()
    tokens = jnp.concatenate([joined(keyb, 0), joined(keyb, 1)], axis=0)
    rows = stacked(unit(tokens, width)[0] * gain)
    kb[...] = stacked(project(rows, 2))
    vb[...] = stacked(project(rows, 3))

    for copy in back_copies2:
        copy.wait_recv()
    dc_ref[...] = joined(back) * gate

    head_of = lax.broadcasted_iota(jnp.int32, (heads, width), 0) * dim
    feature = lax.broadcasted_iota(jnp.int32, (heads, width), 1)
    mask = jnp.where((feature >= head_of) & (feature < head_of + dim), 1.0, 0.0)
    flat = CHUNK * heads

    def by_head(ref, k):
        x = ref[pl.ds(pl.multiple_of(CHUNK * k, CHUNK), CHUNK), :]
        return stacked((x[:, None, :] * mask[None]).reshape(flat, width))

    lane = lax.broadcasted_iota(jnp.int32, (flat, 128), 1)

    def forward(k, carry):
        here = pl.ds(CHUNK * k, CHUNK)
        s = s_ref[here].reshape(flat, -1)
        s = s + dot_rows(by_head(q_ref, k), kb[...])
        top = jnp.max(s, axis=-1, keepdims=True)
        expo = jnp.exp(s - top)
        dp = dot_rows(by_head(dc_ref, k), vb[...])
        sums = jnp.sum(expo, axis=-1, keepdims=True)
        delta = jnp.sum(expo * dp, axis=-1, keepdims=True)
        s_ref[here] = expo.reshape(CHUNK, heads, -1)
        dp_ref[here] = dp.reshape(CHUNK, heads, -1)
        packed = jnp.where(lane == 0, top, jnp.where(lane == 1, sums, delta))
        stat[c, k] = packed.T[:8]
        return carry

    lax.fori_loop(0, n_chunk, forward, 0)
    stat_copies = spread_out(3, lambda d: stat.at[c], lambda d: stat.at[c])
    keys_here = vb.shape[0] // 2

    def weigh(k, carry):
        expo = s_ref[pl.ds(CHUNK * k, CHUNK)].reshape(flat, -1)
        wide = dot_deep(expo, vb[...], vb[:keys_here]).reshape(CHUNK, heads, width)
        ctx_ref[pl.ds(pl.multiple_of(CHUNK * k, CHUNK), CHUNK), :] = jnp.sum(wide * mask[None], axis=1)
        return carry

    lax.fori_loop(0, n_chunk, weigh, 0)
    ctx = ctx_ref[...]
    for b in range(n_col):
        ctx_out[b] = ctx[:, b * blk : (b + 1) * blk]
    ctx_copies = spread_out(4, lambda d: ctx_out.at[peer(d)], lambda d: ctx_in.at[d])
    own_head = lax.broadcasted_iota(jnp.int32, (heads, blk), 0) * dim
    own_feature = lax.broadcasted_iota(jnp.int32, (heads, blk), 1) + c * blk
    own_mask = jnp.where((own_feature >= own_head) & (own_feature < own_head + dim), 1.0, 0.0)
    for copy in stat_copies:
        copy.wait_recv()

    def backward(k, carry):
        here = pl.ds(CHUNK * k, CHUNK)
        every = [stat[b, k] for b in range(n_col)]
        top = functools.reduce(jnp.maximum, [x[0:1] for x in every])
        factors = [jnp.exp(x[0:1] - top) for x in every]
        sums = sum(f * x[1:2] for f, x in zip(factors, every))
        delta = sum(f * x[2:3] for f, x in zip(factors, every)) / sums
        mine = jnp.exp(stat[c, k][0:1] - top) / sums
        sub = lax.broadcasted_iota(jnp.int32, (128, flat), 0)
        columns = jnp.where(sub == 0, mine, delta)
        sources = [stat[peer(n_col - d), k][0:1] for d in range(n_col)]
        for d, x in enumerate(sources):
            columns = jnp.where(sub == 2 + d, jnp.exp(x - top) / sums, columns)
        columns = columns.T
        for d in range(n_col):
            weight = columns[:, 2 + d : 3 + d].reshape(CHUNK, heads, 1) * own_mask[None]
            rows_here = pl.ds(pl.multiple_of(CHUNK * k, CHUNK), CHUNK)
            factor[d, rows_here, :] = jnp.sum(weight, axis=1)
        probs = s_ref[here].reshape(flat, -1) * columns[:, 0:1]
        ds = probs * (dp_ref[here].reshape(flat, -1) - columns[:, 1:2])
        ds = ds.reshape(CHUNK, heads, -1)
        dp_ref[here] = ds
        across = jnp.concatenate([ds[i] for i in range(CHUNK)], axis=1)
        x_hi, x_lo = split(pair_v[here].reshape(-1, channels))
        both = dot(stacked(across), jnp.concatenate([x_hi, x_lo], axis=1), NN)
        carry = carry + (
            both[:heads, :channels] + (both[:heads, channels:] + both[heads:, :channels])
        )
        return carry

    total_w[0] = lax.fori_loop(0, n_chunk, backward, jnp.zeros((heads, channels), F32))
    near_copies = []
    for d in range(1, n_row):
        copy = remote(
            total_w.at[0], near.at[d], sum_send.at[d], sum_recv.at[d], row=(r + d) % n_row
        )
        copy.start()
        near_copies.append(copy)
    total = ctx_out[c] * factor[0]
    for d, copy in enumerate(ctx_copies, 1):
        copy.wait_recv()
        total = total + ctx_in[d] * factor[d]
    gctx[c] = total * gate_b[c]
    gctx_copies = spread_out(5, lambda d: gctx.at[c], lambda d: gctx.at[c])

    def pair_back(k, carry):
        ds = dp_ref[pl.ds(CHUNK * k, CHUNK)]
        columns = ds.reshape(flat, -1).T
        d_unit = dot_deep(columns, wide_b[...], wide_b[:flat])
        for i in range(CHUNK):
            d = d_unit[:, channels * i : channels * (i + 1)]
            x = pair_v[CHUNK * k + i]
            slope = jnp.sum(d * x, axis=-1, keepdims=True) * (1.0 / channels)
            grad_ref[CHUNK * k + i] = (d - x * slope) * scale_v[CHUNK * k + i]
        return carry

    lax.fori_loop(0, n_chunk // 2, pair_back, 0)

    total = total_w[0]
    for d, copy in enumerate(near_copies, 1):
        copy.wait_recv()
        total = total + near[d]
    total_w[1] = total
    far_copies = []
    for d in range(1, n_col):
        k = n_row + d
        copy = remote(total_w.at[1], far.at[d], sum_send.at[k], sum_recv.at[k], col=peer(d))
        copy.start()
        far_copies.append(copy)
    lax.fori_loop(n_chunk // 2, n_chunk, pair_back, 0)

    total = total_w[1]
    for d, copy in enumerate(far_copies, 1):
        copy.wait_recv()
        total = total + far[d]
    bgrad_ref[...] = total * pgain_ref[...]
    for copy in gctx_copies:
        copy.wait_recv()
    att_ref[...] = dot3(stacked(joined(gctx)), *split(wout_ref[...]), NT)

    waits = tok_copies + back_copies + back_copies2 + stat_copies + ctx_copies + gctx_copies
    for copy in waits + near_copies + far_copies:
        copy.wait_send()
    for condition, copy in forwards:
        if condition is None:
            copy.wait_send()
        else:
            pl.when(condition)(copy.wait_send)


def write_kernel(*refs):
    count = len(refs) // 2
    copies = [
        pltpu.make_async_copy(src, dst, refs[-1].at[k])
        for k, (src, dst) in enumerate(zip(refs[:count], refs[count:-1]))
    ]
    for copy in copies:
        copy.start()
    for copy in copies:
        copy.wait()


def local(
    n_row, n_col,
    single, pair, single_gain, pair_gain, w_query, w_key, w_value, w_gate, w_bias, w_out, cotangent
):
    tq, blk = single.shape
    width = single_gain.shape[0]
    channels, heads = w_bias.shape
    keys = pair.shape[1]
    n_chunk = tq // CHUNK
    vmem = pl.BlockSpec(memory_space=pltpu.VMEM)
    hbm = pl.BlockSpec(memory_space=pl.ANY)
    bits = (n_row // 2).bit_length() - 1
    w_bias_t = w_bias.T
    pair_gain = pair_gain.reshape(1, channels)
    blocks = pltpu.VMEM((n_col, tq, blk), F32)
    dma = pltpu.SemaphoreType.DMA
    attended, pair_grad, bias_grad = pl.pallas_call(
        functools.partial(layer_kernel, n_row, n_col, heads),
        out_shape=(
            pltpu.VMEM((tq, blk), F32),
            pltpu.VMEM(pair.shape, F32),
            pltpu.VMEM((heads, channels), F32),
        ),
        in_specs=[vmem, hbm, vmem, vmem, hbm, hbm, hbm, hbm, vmem, vmem, vmem],
        out_specs=(vmem,) * 3,
        scratch_shapes=[
            pltpu.VMEM(pair.shape, F32),
            pltpu.VMEM(pair.shape, F32),
            *[pltpu.VMEM((width, width), F32)] * 4,
            blocks,
            pltpu.VMEM((2, n_col, tq, blk), F32),
            blocks, blocks, blocks,
            pltpu.VMEM((tq, heads, keys), F32),
            pltpu.VMEM((tq, heads, keys), F32),
            pltpu.VMEM((tq, width), F32),
            pltpu.VMEM((tq, width), F32),
            blocks,
            *[pltpu.VMEM((2 * keys, width), BF16)] * 2,
            pltpu.VMEM((n_col, n_chunk, 8, CHUNK * heads), F32),
            pltpu.VMEM((tq, width), F32),
            blocks, blocks, blocks,
            *[pltpu.VMEM((4, width, width), BF16)] * 2,
            pltpu.VMEM((2 * CHUNK * heads, CHUNK * channels), BF16),
            pltpu.VMEM((2, heads, channels), F32),
            pltpu.VMEM((n_row, heads, channels), F32),
            pltpu.VMEM((n_col, heads, channels), F32),
            blocks,
            dma((n_row + n_col,)), dma((n_row + n_col,)),
            dma((4,)), dma((n_chunk,)), dma((6, n_col)), dma((6, n_col)),
            dma((bits, n_col)), dma((n_col,)), dma((n_col,)), dma((n_col,)),
        ],
        compiler_params=pltpu.CompilerParams(
            collective_id=0, has_side_effects=True, vmem_limit_bytes=VMEM_LIMIT
        ),
        name="layer",
    )(
        single, pair, single_gain, pair_gain, w_query, w_key, w_value, w_gate, w_bias_t, w_out.T,
        cotangent,
    )
    results = (attended, pair_grad, bias_grad)
    attended, pair_grad, bias_grad = pl.pallas_call(
        write_kernel,
        out_shape=tuple(jax.ShapeDtypeStruct(x.shape, F32) for x in results),
        in_specs=[vmem] * 3,
        out_specs=(hbm,) * 3,
        scratch_shapes=[dma((3,))],
        compiler_params=pltpu.CompilerParams(vmem_limit_bytes=1024 * 1024),
        name="write_out",
    )(*[pltpu.with_memory_space_constraint(x, pltpu.VMEM) for x in results])
    return (attended, pair_grad, bias_grad.T)


def solution(mesh):
    placed = (
        P("row", "col"),
        P("row", "col", None),
        P(),
        P(),
        P(),
        P(),
        P(),
        P(),
        P(),
        P(None, "col"),
        P("row", "col"),
    )
    return jax.shard_map(
        functools.partial(local, mesh.shape["row"], mesh.shape["col"]),
        mesh=mesh,
        in_specs=placed,
        out_specs=(P("row", "col"), P("row", "col", None), P()),
        check_vma=False,
    )
```

```python
import functools

import jax
import jax.numpy as jnp
from jax import lax
from jax.experimental import pallas as pl
from jax.experimental.pallas import tpu as pltpu
from jax.sharding import PartitionSpec as P

MESH = pl.DeviceIdType.MESH
VMEM_LIMIT = 48 * 1024 * 1024
CHUNK = 8
F32 = jnp.float32
BF16 = jnp.bfloat16
NN = (((1,), (0,)), ((), ()))
NT = (((1,), (1,)), ((), ()))


def split(x):
    hi = x.astype(BF16)
    return hi, (x - hi.astype(F32)).astype(BF16)


def stacked(x):
    return jnp.concatenate(split(x), axis=0)


def dot(a, b, dims):
    return lax.dot_general(a, b, dims, preferred_element_type=F32)


def dot3(both, b_hi, b_lo, dims):
    m = both.shape[0] // 2
    high = dot(both, b_hi, dims)
    return high[:m] + high[m:] + dot(both[:m], b_lo, dims)


def dot_rows(both, b_both):
    m, n = both.shape[0] // 2, b_both.shape[0] // 2
    out = dot(both, b_both, NT)
    return out[:m, :n] + (out[:m, n:] + out[m:, :n])


def dot_deep(x, b_both, b_hi):
    hi, lo = split(x)
    return dot(jnp.concatenate([hi, hi], axis=1), b_both, NN) + dot(lo, b_hi, NN)


def unit(x, width):
    centre = jnp.sum(x, axis=-1, keepdims=True) * (1.0 / width)
    x = x - centre
    spread = jnp.sum(x * x, axis=-1, keepdims=True) * (1.0 / width)
    scale = lax.rsqrt(spread + 1e-05)
    return x * scale, scale


def remote(src, dst, send_sem, recv_sem, **device):
    return pltpu.make_async_remote_copy(
        src_ref=src, dst_ref=dst, send_sem=send_sem, recv_sem=recv_sem,
        device_id=device, device_id_type=MESH,
    )


def greet(devices):
    barrier = pltpu.get_barrier_semaphore()
    for device in devices:
        pl.semaphore_signal(barrier, inc=1, device_id=device, device_id_type=MESH)
    pl.semaphore_wait(barrier, len(devices))


def in_pairs(start, stop, body, carry):
    def two(k, carry):
        for u in range(2):
            carry = body(2 * k + u, carry)
        return carry

    return lax.fori_loop(start // 2, stop // 2, two, carry)


def layer_kernel(
    n_row, n_col, heads,
    single_hbm, pair_hbm, gain_hbm, pgain_hbm, wq_hbm, wk_hbm, wv_hbm, wg_hbm, wbt_hbm, wout_hbm,
    cot_hbm,
    att_ref, grad_ref, bgrad_ref,
    pair_v, scale_v, wq_v, wk_v, wv_v, wg_v,
    tok, keyb, part_out, part_in, back, s_ref, dp_ref, q_ref, dc_ref, gate_b,
    kb, vb, stat, ctx_ref, ctx_out, ctx_in, gctx,
    w_hi, w_lo, wide_b, total_w, near, far, factor,
    cot_ref, wout_ref, wbt_ref, pgain_ref, gain_ref,
    i_sem, sum_send, sum_recv, w_sem, p_sem, send_sem, recv_sem, tree_send, tree_recv, mate_send, mate_recv,
):
    r = lax.axis_index("row")
    c = lax.axis_index("col")
    tq, blk = single_hbm.shape
    width = blk * n_col
    dim = width // heads
    n_chunk = tq // CHUNK
    n_chip = n_row // 2
    bits = n_chip.bit_length() - 1
    parity = r % 2
    chip = r // 2

    weights = [(wq_hbm, wq_v), (wg_hbm, wg_v), (wk_hbm, wk_v), (wv_hbm, wv_v)]
    pair_copies = [
        pltpu.make_async_copy(
            pair_hbm.at[pl.ds(CHUNK * k, CHUNK)], pair_v.at[pl.ds(CHUNK * k, CHUNK)], p_sem.at[k]
        )
        for k in range(n_chunk)
    ]
    weight_copies = [
        pltpu.make_async_copy(src, dst, w_sem.at[k]) for k, (src, dst) in enumerate(weights)
    ]
    small = [
        (single_hbm, tok.at[c]), (cot_hbm, cot_ref), (wout_hbm, wout_ref),
        (wbt_hbm, wbt_ref), (pgain_hbm, pgain_ref), (gain_hbm, gain_ref),
    ]
    small_copies = [
        pltpu.make_async_copy(src, dst, i_sem.at[k]) for k, (src, dst) in enumerate(small)
    ]
    for copy in small_copies + pair_copies[:2] + weight_copies + pair_copies[2:]:
        copy.start()

    def peer(d):
        return (c + d) % n_col

    mate = r + 1 - 2 * parity
    chip_bits = [(chip // (1 << e)) % 2 for e in range(bits)]
    col_bits = [(c // (1 << e)) % 2 for e in range(bits)]
    away = [a + b - 2 * a * b for a, b in zip(chip_bits, col_bits)]
    beside = [r + (2 << e) * (1 - 2 * chip_bits[e]) for e in range(bits)]
    greet(
        [{"col": peer(d)} for d in range(1, n_col)]
        + [{"row": (r + d) % n_row} for d in range(1, n_row)]
    )

    def spread_out(stage, src_of, dst_of):
        copies = []
        for d in range(1, n_col):
            copy = remote(
                src_of(d), dst_of(d), send_sem.at[stage, d], recv_sem.at[stage, d], col=peer(d)
            )
            copy.start()
            copies.append(copy)
        return copies

    small_copies[0].wait()
    tok_copies = spread_out(0, lambda d: tok.at[c], lambda d: tok.at[c])
    for copy in small_copies[1:]:
        copy.wait()

    part = dot3(stacked(cot_ref[...]), *split(wout_ref[...]), NN)
    for b in range(n_col):
        part_out[b] = part[:, b * blk : (b + 1) * blk]
    gain = gain_ref[...].reshape(1, width)

    weight_t = wbt_ref[...] * pgain_ref[...]
    wb = stacked(weight_t)
    wb = jnp.concatenate([wb, jnp.concatenate([wb[:heads], jnp.zeros_like(wb[:heads])], 0)], 1)

    def pair_bias(k):
        pair_copies[k].wait()
        x = pair_v[pl.ds(CHUNK * k, CHUNK)]
        x, scale = unit(x, x.shape[-1])
        pair_v[pl.ds(CHUNK * k, CHUNK)] = x
        scale_v[pl.ds(CHUNK * k, CHUNK)] = jnp.broadcast_to(scale, x.shape)
        bias = dot(wb, jnp.concatenate(split(x.reshape(-1, x.shape[-1])), axis=1), NT)
        bias = bias[:heads] + bias[heads:]
        keys_here = s_ref.shape[2]
        for i in range(CHUNK):
            s_ref[CHUNK * k + i] = bias[:, i * keys_here : (i + 1) * keys_here]

    at_source = sum(away) == 0
    forwards = []
    for t in range(n_col):
        block = (c - t + n_col) % n_col
        if t:
            tok_copies[t - 1].wait_recv()

        @pl.when(at_source)
        def _():
            keyb[parity, block] = tok[block]

        @pl.when(jnp.logical_not(at_source))
        def _():
            remote(
                keyb.at[parity, block], keyb.at[parity, block], tree_send.at[0, t],
                tree_recv.at[t], row=mate,
            ).wait_recv()

        for e in reversed(range(bits)):
            copy = remote(
                keyb.at[parity, block], keyb.at[parity, block], tree_send.at[e, t],
                tree_recv.at[t], row=beside[e],
            )
            forwards.append((sum(away[: e + 1]) == 0, copy))
            pl.when(forwards[-1][0])(copy.start)
        copy = remote(
            keyb.at[parity, block], keyb.at[parity, block], mate_send.at[t], mate_recv.at[t],
            row=mate,
        )
        copy.start()
        forwards.append((None, copy))
        if t == n_col - 2:
            back_copies = spread_out(1, lambda d: part_out.at[peer(d)], lambda d: part_in.at[d])
        if t < n_col - 1:
            early = n_chunk - 3
            for k in range(t * early // (n_col - 1), (t + 1) * early // (n_col - 1)):
                pair_bias(k)

    for copy in back_copies:
        copy.wait_recv()
    total = part_out[c]
    for d in range(1, n_col):
        total = total + part_in[d]
    back[c] = total
    back_copies2 = spread_out(2, lambda d: back.at[c], lambda d: back.at[c])

    for k in range(n_chunk - 3, n_chunk):
        pair_bias(k)
    step = 256
    for k, (_, w_ref) in enumerate(weights):
        weight_copies[k].wait()
        for lo in range(0, width, step):
            w_hi[k, lo : lo + step], w_lo[k, lo : lo + step] = split(w_ref[lo : lo + step, :])
    wide_b[...] = jnp.zeros_like(wide_b)
    centred = weight_t - jnp.sum(weight_t, axis=1, keepdims=True) * (1.0 / weight_t.shape[1])
    channels = weight_t.shape[1]
    for half, value in enumerate(split(centred)):
        for i in range(CHUNK):
            row = half * CHUNK * heads + heads * i
            wide_b[row : row + heads, channels * i : channels * (i + 1)] = value

    def project(both, k):
        out = None
        for lo in range(0, width, step):
            piece = dot3(
                both[:, lo : lo + step], w_hi[k, lo : lo + step], w_lo[k, lo : lo + step], NN
            )
            out = piece if out is None else out + piece
        return out

    def joined(ref, *lead):
        return jnp.concatenate([ref[(*lead, b)] for b in range(n_col)], axis=1)

    rows = stacked(unit(joined(tok), width)[0] * gain)
    q_ref[...] = project(rows, 0) * dim ** (-0.5)
    gate = jax.nn.sigmoid(project(rows, 1))
    for b in range(n_col):
        gate_b[b] = gate[:, b * blk : (b + 1) * blk]

    for _, copy in forwards[bits :: bits + 1]:
        copy.wait_recv()
    tokens = jnp.concatenate([joined(keyb, 0), joined(keyb, 1)], axis=0)
    rows = stacked(unit(tokens, width)[0] * gain)
    kb[...] = stacked(project(rows, 2))
    vb[...] = stacked(project(rows, 3))

    for copy in back_copies2:
        copy.wait_recv()
    dc_ref[...] = joined(back) * gate

    head_of = lax.broadcasted_iota(jnp.int32, (heads, width), 0) * dim
    feature = lax.broadcasted_iota(jnp.int32, (heads, width), 1)
    mask = jnp.where((feature >= head_of) & (feature < head_of + dim), 1.0, 0.0)
    flat = CHUNK * heads

    def by_head(ref, k):
        x = ref[pl.ds(pl.multiple_of(CHUNK * k, CHUNK), CHUNK), :]
        return stacked((x[:, None, :] * mask[None]).reshape(flat, width))

    lane = lax.broadcasted_iota(jnp.int32, (flat, 128), 1)

    def forward(k, carry):
        here = pl.ds(CHUNK * k, CHUNK)
        s = s_ref[here].reshape(flat, -1)
        s = s + dot_rows(by_head(q_ref, k), kb[...])
        top = jnp.max(s, axis=-1, keepdims=True)
        expo = jnp.exp(s - top)
        dp = dot_rows(by_head(dc_ref, k), vb[...])
        sums = jnp.sum(expo, axis=-1, keepdims=True)
        delta = jnp.sum(expo * dp, axis=-1, keepdims=True)
        s_ref[here] = expo.reshape(CHUNK, heads, -1)
        dp_ref[here] = dp.reshape(CHUNK, heads, -1)
        packed = jnp.where(lane == 0, top, jnp.where(lane == 1, sums, delta))
        stat[c, k] = packed.T[:8]
        return carry

    in_pairs(0, n_chunk, forward, 0)
    stat_copies = spread_out(3, lambda d: stat.at[c], lambda d: stat.at[c])
    keys_here = vb.shape[0] // 2

    def weigh(k, carry):
        expo = s_ref[pl.ds(CHUNK * k, CHUNK)].reshape(flat, -1)
        wide = dot_deep(expo, vb[...], vb[:keys_here]).reshape(CHUNK, heads, width)
        ctx_ref[pl.ds(pl.multiple_of(CHUNK * k, CHUNK), CHUNK), :] = jnp.sum(wide * mask[None], axis=1)
        return carry

    in_pairs(0, n_chunk, weigh, 0)
    ctx = ctx_ref[...]
    for b in range(n_col):
        ctx_out[b] = ctx[:, b * blk : (b + 1) * blk]
    ctx_copies = spread_out(4, lambda d: ctx_out.at[peer(d)], lambda d: ctx_in.at[d])
    own_head = lax.broadcasted_iota(jnp.int32, (heads, blk), 0) * dim
    own_feature = lax.broadcasted_iota(jnp.int32, (heads, blk), 1) + c * blk
    own_mask = jnp.where((own_feature >= own_head) & (own_feature < own_head + dim), 1.0, 0.0)
    for copy in stat_copies:
        copy.wait_recv()

    def backward(k, carry):
        here = pl.ds(CHUNK * k, CHUNK)
        every = [stat[b, k] for b in range(n_col)]
        top = functools.reduce(jnp.maximum, [x[0:1] for x in every])
        factors = [jnp.exp(x[0:1] - top) for x in every]
        sums = sum(f * x[1:2] for f, x in zip(factors, every))
        delta = sum(f * x[2:3] for f, x in zip(factors, every)) / sums
        mine = jnp.exp(stat[c, k][0:1] - top) / sums
        sub = lax.broadcasted_iota(jnp.int32, (128, flat), 0)
        columns = jnp.where(sub == 0, mine, delta)
        sources = [stat[peer(n_col - d), k][0:1] for d in range(n_col)]
        for d, x in enumerate(sources):
            columns = jnp.where(sub == 2 + d, jnp.exp(x - top) / sums, columns)
        columns = columns.T
        for d in range(n_col):
            weight = columns[:, 2 + d : 3 + d].reshape(CHUNK, heads, 1) * own_mask[None]
            rows_here = pl.ds(pl.multiple_of(CHUNK * k, CHUNK), CHUNK)
            factor[d, rows_here, :] = jnp.sum(weight, axis=1)
        probs = s_ref[here].reshape(flat, -1) * columns[:, 0:1]
        ds = probs * (dp_ref[here].reshape(flat, -1) - columns[:, 1:2])
        ds = ds.reshape(CHUNK, heads, -1)
        dp_ref[here] = ds
        across = jnp.concatenate([ds[i] for i in range(CHUNK)], axis=1)
        x_hi, x_lo = split(pair_v[here].reshape(-1, channels))
        both = dot(stacked(across), jnp.concatenate([x_hi, x_lo], axis=1), NN)
        carry = carry + (
            both[:heads, :channels] + (both[:heads, channels:] + both[heads:, :channels])
        )
        return carry

    total_w[0] = in_pairs(0, n_chunk, backward, jnp.zeros((heads, channels), F32))
    near_copies = []
    for d in range(1, n_row):
        copy = remote(
            total_w.at[0], near.at[d], sum_send.at[d], sum_recv.at[d], row=(r + d) % n_row
        )
        copy.start()
        near_copies.append(copy)
    total = ctx_out[c] * factor[0]
    for d, copy in enumerate(ctx_copies, 1):
        copy.wait_recv()
        total = total + ctx_in[d] * factor[d]
    gctx[c] = total * gate_b[c]
    gctx_copies = spread_out(5, lambda d: gctx.at[c], lambda d: gctx.at[c])

    def pair_back(k, carry):
        ds = dp_ref[pl.ds(CHUNK * k, CHUNK)]
        columns = ds.reshape(flat, -1).T
        d_unit = dot_deep(columns, wide_b[...], wide_b[:flat])
        for i in range(CHUNK):
            d = d_unit[:, channels * i : channels * (i + 1)]
            x = pair_v[CHUNK * k + i]
            slope = jnp.sum(d * x, axis=-1, keepdims=True) * (1.0 / channels)
            grad_ref[CHUNK * k + i] = (d - x * slope) * scale_v[CHUNK * k + i]
        return carry

    in_pairs(0, n_chunk // 2, pair_back, 0)

    total = total_w[0]
    for d, copy in enumerate(near_copies, 1):
        copy.wait_recv()
        total = total + near[d]
    total_w[1] = total
    far_copies = []
    for d in range(1, n_col):
        k = n_row + d
        copy = remote(total_w.at[1], far.at[d], sum_send.at[k], sum_recv.at[k], col=peer(d))
        copy.start()
        far_copies.append(copy)
    in_pairs(n_chunk // 2, n_chunk, pair_back, 0)

    total = total_w[1]
    for d, copy in enumerate(far_copies, 1):
        copy.wait_recv()
        total = total + far[d]
    bgrad_ref[...] = total * pgain_ref[...]
    for copy in gctx_copies:
        copy.wait_recv()
    att_ref[...] = dot3(stacked(joined(gctx)), *split(wout_ref[...]), NT)

    waits = tok_copies + back_copies + back_copies2 + stat_copies + ctx_copies + gctx_copies
    for copy in waits + near_copies + far_copies:
        copy.wait_send()
    for condition, copy in forwards:
        if condition is None:
            copy.wait_send()
        else:
            pl.when(condition)(copy.wait_send)


def write_kernel(*refs):
    count = len(refs) // 2
    copies = [
        pltpu.make_async_copy(src, dst, refs[-1].at[k])
        for k, (src, dst) in enumerate(zip(refs[:count], refs[count:-1]))
    ]
    for copy in copies:
        copy.start()
    for copy in copies:
        copy.wait()


def local(
    n_row, n_col,
    single, pair, single_gain, pair_gain, w_query, w_key, w_value, w_gate, w_bias, w_out, cotangent
):
    tq, blk = single.shape
    width = single_gain.shape[0]
    channels, heads = w_bias.shape
    keys = pair.shape[1]
    n_chunk = tq // CHUNK
    vmem = pl.BlockSpec(memory_space=pltpu.VMEM)
    hbm = pl.BlockSpec(memory_space=pltpu.HBM)
    bits = (n_row // 2).bit_length() - 1
    w_bias_t = w_bias.T
    pair_gain = pair_gain.reshape(1, channels)
    blocks = pltpu.VMEM((n_col, tq, blk), F32)
    dma = pltpu.SemaphoreType.DMA
    attended, pair_grad, bias_grad = pl.pallas_call(
        functools.partial(layer_kernel, n_row, n_col, heads),
        out_shape=(
            pltpu.VMEM((tq, blk), F32),
            pltpu.VMEM(pair.shape, F32),
            pltpu.VMEM((heads, channels), F32),
        ),
        in_specs=[hbm] * 11,
        out_specs=(vmem,) * 3,
        scratch_shapes=[
            pltpu.VMEM(pair.shape, F32),
            pltpu.VMEM(pair.shape, F32),
            *[pltpu.VMEM((width, width), F32)] * 4,
            blocks,
            pltpu.VMEM((2, n_col, tq, blk), F32),
            blocks, blocks, blocks,
            pltpu.VMEM((tq, heads, keys), F32),
            pltpu.VMEM((tq, heads, keys), F32),
            pltpu.VMEM((tq, width), F32),
            pltpu.VMEM((tq, width), F32),
            blocks,
            *[pltpu.VMEM((2 * keys, width), BF16)] * 2,
            pltpu.VMEM((n_col, n_chunk, 8, CHUNK * heads), F32),
            pltpu.VMEM((tq, width), F32),
            blocks, blocks, blocks,
            *[pltpu.VMEM((4, width, width), BF16)] * 2,
            pltpu.VMEM((2 * CHUNK * heads, CHUNK * channels), BF16),
            pltpu.VMEM((2, heads, channels), F32),
            pltpu.VMEM((n_row, heads, channels), F32),
            pltpu.VMEM((n_col, heads, channels), F32),
            blocks,
            pltpu.VMEM((tq, blk), F32),
            pltpu.VMEM((blk, width), F32),
            pltpu.VMEM((heads, channels), F32),
            pltpu.VMEM((1, channels), F32),
            pltpu.VMEM((width,), F32),
            dma((6,)),
            dma((n_row + n_col,)), dma((n_row + n_col,)),
            dma((4,)), dma((n_chunk,)), dma((6, n_col)), dma((6, n_col)),
            dma((bits, n_col)), dma((n_col,)), dma((n_col,)), dma((n_col,)),
        ],
        compiler_params=pltpu.CompilerParams(
            collective_id=0, has_side_effects=True, vmem_limit_bytes=VMEM_LIMIT
        ),
        name="layer",
    )(
        *[
            pltpu.with_memory_space_constraint(x, pltpu.HBM)
            for x in (
                single, pair, single_gain, pair_gain, w_query, w_key, w_value, w_gate, w_bias_t,
                w_out.T, cotangent,
            )
        ]
    )
    results = (attended, pair_grad, bias_grad)
    attended, pair_grad, bias_grad = pl.pallas_call(
        write_kernel,
        out_shape=tuple(jax.ShapeDtypeStruct(x.shape, F32) for x in results),
        in_specs=[vmem] * 3,
        out_specs=(hbm,) * 3,
        scratch_shapes=[dma((3,))],
        compiler_params=pltpu.CompilerParams(vmem_limit_bytes=1024 * 1024),
        name="write_out",
    )(*[pltpu.with_memory_space_constraint(x, pltpu.VMEM) for x in results])
    return (attended, pair_grad, bias_grad.T)


def solution(mesh):
    placed = (
        P("row", "col"),
        P("row", "col", None),
        P(),
        P(),
        P(),
        P(),
        P(),
        P(),
        P(),
        P(None, "col"),
        P("row", "col"),
    )
    return jax.shard_map(
        functools.partial(local, mesh.shape["row"], mesh.shape["col"]),
        mesh=mesh,
        in_specs=placed,
        out_specs=(P("row", "col"), P("row", "col", None), P()),
        check_vma=False,
    )
```

```python
import functools

import jax
import jax.numpy as jnp
from jax import lax
from jax.experimental import pallas as pl
from jax.experimental.pallas import tpu as pltpu
from jax.sharding import PartitionSpec as P

MESH = pl.DeviceIdType.MESH
VMEM_LIMIT = 48 * 1024 * 1024
CHUNK = 8
F32 = jnp.float32
BF16 = jnp.bfloat16
NN = (((1,), (0,)), ((), ()))
NT = (((1,), (1,)), ((), ()))


def split(x):
    hi = x.astype(BF16)
    return hi, (x - hi.astype(F32)).astype(BF16)


def stacked(x):
    return jnp.concatenate(split(x), axis=0)


def dot(a, b, dims):
    return lax.dot_general(a, b, dims, preferred_element_type=F32)


def dot3(both, b_hi, b_lo, dims):
    m = both.shape[0] // 2
    high = dot(both, b_hi, dims)
    return high[:m] + high[m:] + dot(both[:m], b_lo, dims)


def dot_rows(both, b_both):
    m, n = both.shape[0] // 2, b_both.shape[0] // 2
    out = dot(both, b_both, NT)
    return out[:m, :n] + (out[:m, n:] + out[m:, :n])


def dot_deep(x, b_both, b_hi):
    hi, lo = split(x)
    return dot(jnp.concatenate([hi, hi], axis=1), b_both, NN) + dot(lo, b_hi, NN)


def unit(x, width):
    centre = jnp.sum(x, axis=-1, keepdims=True) * (1.0 / width)
    x = x - centre
    spread = jnp.sum(x * x, axis=-1, keepdims=True) * (1.0 / width)
    scale = lax.rsqrt(spread + 1e-05)
    return x * scale, scale


def remote(src, dst, send_sem, recv_sem, **device):
    return pltpu.make_async_remote_copy(
        src_ref=src, dst_ref=dst, send_sem=send_sem, recv_sem=recv_sem,
        device_id=device, device_id_type=MESH,
    )


def greet(devices):
    barrier = pltpu.get_barrier_semaphore()
    for device in devices:
        pl.semaphore_signal(barrier, inc=1, device_id=device, device_id_type=MESH)
    pl.semaphore_wait(barrier, len(devices))


def in_pairs(start, stop, body, carry):
    def two(k, carry):
        for u in range(2):
            carry = body(2 * k + u, carry)
        return carry

    return lax.fori_loop(start // 2, stop // 2, two, carry)


def layer_kernel(
    n_row, n_col, heads,
    single_hbm, pair_hbm, gain_hbm, pgain_hbm, wq_hbm, wk_hbm, wv_hbm, wg_hbm, wbt_hbm, wout_hbm,
    cot_hbm,
    att_ref, grad_ref, bgrad_ref,
    pair_v, scale_v, wq_v, wk_v, wv_v, wg_v,
    tok, keyb, part_out, part_in, back, s_ref, dp_ref, q_ref, dc_ref, gate_b,
    kb, vb, stat, ctx_ref, ctx_out, ctx_in, gctx,
    w_hi, w_lo, wide_b, total_w, near, far, factor,
    cot_ref, wout_ref, wbt_ref, pgain_ref, gain_ref,
    i_sem, sum_send, sum_recv, w_sem, p_sem, send_sem, recv_sem, tree_send, tree_recv, mate_send, mate_recv,
):
    r = lax.axis_index("row")
    c = lax.axis_index("col")
    tq, blk = single_hbm.shape
    width = blk * n_col
    dim = width // heads
    n_chunk = tq // CHUNK
    n_chip = n_row // 2
    bits = n_chip.bit_length() - 1
    parity = r % 2
    chip = r // 2

    weights = [(wq_hbm, wq_v), (wg_hbm, wg_v), (wk_hbm, wk_v), (wv_hbm, wv_v)]
    pair_copies = [
        pltpu.make_async_copy(
            pair_hbm.at[pl.ds(CHUNK * k, CHUNK)], pair_v.at[pl.ds(CHUNK * k, CHUNK)], p_sem.at[k]
        )
        for k in range(n_chunk)
    ]
    weight_copies = [
        pltpu.make_async_copy(src, dst, w_sem.at[k]) for k, (src, dst) in enumerate(weights)
    ]
    small = [
        (single_hbm, tok.at[c]), (cot_hbm, cot_ref), (wout_hbm, wout_ref),
        (wbt_hbm, wbt_ref), (pgain_hbm, pgain_ref), (gain_hbm, gain_ref),
    ]
    small_copies = [
        pltpu.make_async_copy(src, dst, i_sem.at[k]) for k, (src, dst) in enumerate(small)
    ]
    for copy in small_copies + pair_copies[:2] + weight_copies + pair_copies[2:]:
        copy.start()

    def peer(d):
        return (c + d) % n_col

    mate = r + 1 - 2 * parity
    chip_bits = [(chip // (1 << e)) % 2 for e in range(bits)]
    col_bits = [(c // (1 << e)) % 2 for e in range(bits)]
    away = [a + b - 2 * a * b for a, b in zip(chip_bits, col_bits)]
    beside = [r + (2 << e) * (1 - 2 * chip_bits[e]) for e in range(bits)]
    greet(
        [{"col": peer(d)} for d in range(1, n_col)]
        + [{"row": (r + d) % n_row} for d in range(1, n_row)]
    )

    def spread_out(stage, src_of, dst_of):
        copies = []
        for d in range(1, n_col):
            copy = remote(
                src_of(d), dst_of(d), send_sem.at[stage, d], recv_sem.at[stage, d], col=peer(d)
            )
            copy.start()
            copies.append(copy)
        return copies

    small_copies[0].wait()
    tok_copies = spread_out(0, lambda d: tok.at[c], lambda d: tok.at[c])
    for copy in small_copies[1:]:
        copy.wait()

    part = dot3(stacked(cot_ref[...]), *split(wout_ref[...]), NN)
    for b in range(n_col):
        part_out[b] = part[:, b * blk : (b + 1) * blk]
    gain = gain_ref[...].reshape(1, width)

    weight_t = wbt_ref[...] * pgain_ref[...]
    wb = stacked(weight_t)
    wb = jnp.concatenate([wb, jnp.concatenate([wb[:heads], jnp.zeros_like(wb[:heads])], 0)], 1)

    def pair_bias(k):
        pair_copies[k].wait()
        x = pair_v[pl.ds(CHUNK * k, CHUNK)]
        x, scale = unit(x, x.shape[-1])
        pair_v[pl.ds(CHUNK * k, CHUNK)] = x
        scale_v[pl.ds(CHUNK * k, CHUNK)] = jnp.broadcast_to(scale, x.shape)
        bias = dot(wb, jnp.concatenate(split(x.reshape(-1, x.shape[-1])), axis=1), NT)
        bias = bias[:heads] + bias[heads:]
        keys_here = s_ref.shape[2]
        for i in range(CHUNK):
            s_ref[CHUNK * k + i] = bias[:, i * keys_here : (i + 1) * keys_here]

    at_source = sum(away) == 0
    early = min(n_col - 1, n_chunk)
    forwards = []
    for t in range(n_col):
        block = (c - t + n_col) % n_col
        if t:
            tok_copies[t - 1].wait_recv()

        @pl.when(at_source)
        def _():
            keyb[parity, block] = tok[block]

        @pl.when(jnp.logical_not(at_source))
        def _():
            remote(
                keyb.at[parity, block], keyb.at[parity, block], tree_send.at[0, t],
                tree_recv.at[t], row=mate,
            ).wait_recv()

        for e in reversed(range(bits)):
            copy = remote(
                keyb.at[parity, block], keyb.at[parity, block], tree_send.at[e, t],
                tree_recv.at[t], row=beside[e],
            )
            forwards.append((sum(away[: e + 1]) == 0, copy))
            pl.when(forwards[-1][0])(copy.start)
        copy = remote(
            keyb.at[parity, block], keyb.at[parity, block], mate_send.at[t], mate_recv.at[t],
            row=mate,
        )
        copy.start()
        forwards.append((None, copy))
        if t == n_col - 2:
            back_copies = spread_out(1, lambda d: part_out.at[peer(d)], lambda d: part_in.at[d])
        if t < n_col - 1:
            for k in range(t * early // (n_col - 1), (t + 1) * early // (n_col - 1)):
                pair_bias(k)

    for copy in back_copies:
        copy.wait_recv()
    total = part_out[c]
    for d in range(1, n_col):
        total = total + part_in[d]
    back[c] = total
    back_copies2 = spread_out(2, lambda d: back.at[c], lambda d: back.at[c])

    for k in range(early, n_chunk):
        pair_bias(k)
    step = 256
    for k, (_, w_ref) in enumerate(weights):
        weight_copies[k].wait()
        for lo in range(0, width, step):
            w_hi[k, lo : lo + step], w_lo[k, lo : lo + step] = split(w_ref[lo : lo + step, :])
    wide_b[...] = jnp.zeros_like(wide_b)
    centred = weight_t - jnp.sum(weight_t, axis=1, keepdims=True) * (1.0 / weight_t.shape[1])
    channels = weight_t.shape[1]
    for half, value in enumerate(split(centred)):
        for i in range(CHUNK):
            row = half * CHUNK * heads + heads * i
            wide_b[row : row + heads, channels * i : channels * (i + 1)] = value

    def project(both, k):
        out = None
        for lo in range(0, width, step):
            piece = dot3(
                both[:, lo : lo + step], w_hi[k, lo : lo + step], w_lo[k, lo : lo + step], NN
            )
            out = piece if out is None else out + piece
        return out

    def joined(ref, *lead):
        return jnp.concatenate([ref[(*lead, b)] for b in range(n_col)], axis=1)

    rows = stacked(unit(joined(tok), width)[0] * gain)
    q_ref[...] = project(rows, 0) * dim ** (-0.5)
    gate = jax.nn.sigmoid(project(rows, 1))
    for b in range(n_col):
        gate_b[b] = gate[:, b * blk : (b + 1) * blk]

    for _, copy in forwards[bits :: bits + 1]:
        copy.wait_recv()
    tokens = jnp.concatenate([joined(keyb, 0), joined(keyb, 1)], axis=0)
    rows = stacked(unit(tokens, width)[0] * gain)
    kb[...] = stacked(project(rows, 2))
    vb[...] = stacked(project(rows, 3))

    for copy in back_copies2:
        copy.wait_recv()
    dc_ref[...] = joined(back) * gate

    head_of = lax.broadcasted_iota(jnp.int32, (heads, width), 0) * dim
    feature = lax.broadcasted_iota(jnp.int32, (heads, width), 1)
    mask = jnp.where((feature >= head_of) & (feature < head_of + dim), 1.0, 0.0)
    flat = CHUNK * heads

    def by_head(ref, k):
        x = ref[pl.ds(pl.multiple_of(CHUNK * k, CHUNK), CHUNK), :]
        return stacked((x[:, None, :] * mask[None]).reshape(flat, width))

    lane = lax.broadcasted_iota(jnp.int32, (flat, 128), 1)

    def forward(k, carry):
        here = pl.ds(CHUNK * k, CHUNK)
        s = s_ref[here].reshape(flat, -1)
        s = s + dot_rows(by_head(q_ref, k), kb[...])
        top = jnp.max(s, axis=-1, keepdims=True)
        expo = jnp.exp(s - top)
        dp = dot_rows(by_head(dc_ref, k), vb[...])
        sums = jnp.sum(expo, axis=-1, keepdims=True)
        delta = jnp.sum(expo * dp, axis=-1, keepdims=True)
        s_ref[here] = expo.reshape(CHUNK, heads, -1)
        dp_ref[here] = dp.reshape(CHUNK, heads, -1)
        packed = jnp.where(lane == 0, top, jnp.where(lane == 1, sums, delta))
        stat[c, k] = packed.T[:8]
        return carry

    in_pairs(0, n_chunk, forward, 0)
    stat_copies = spread_out(3, lambda d: stat.at[c], lambda d: stat.at[c])
    keys_here = vb.shape[0] // 2

    def weigh(k, carry):
        expo = s_ref[pl.ds(CHUNK * k, CHUNK)].reshape(flat, -1)
        wide = dot_deep(expo, vb[...], vb[:keys_here]).reshape(CHUNK, heads, width)
        ctx_ref[pl.ds(pl.multiple_of(CHUNK * k, CHUNK), CHUNK), :] = jnp.sum(wide * mask[None], axis=1)
        return carry

    in_pairs(0, n_chunk, weigh, 0)
    ctx = ctx_ref[...]
    for b in range(n_col):
        ctx_out[b] = ctx[:, b * blk : (b + 1) * blk]
    ctx_copies = spread_out(4, lambda d: ctx_out.at[peer(d)], lambda d: ctx_in.at[d])
    own_head = lax.broadcasted_iota(jnp.int32, (heads, blk), 0) * dim
    own_feature = lax.broadcasted_iota(jnp.int32, (heads, blk), 1) + c * blk
    own_mask = jnp.where((own_feature >= own_head) & (own_feature < own_head + dim), 1.0, 0.0)
    for copy in stat_copies:
        copy.wait_recv()

    def backward(k, carry):
        here = pl.ds(CHUNK * k, CHUNK)
        every = [stat[b, k] for b in range(n_col)]
        top = functools.reduce(jnp.maximum, [x[0:1] for x in every])
        factors = [jnp.exp(x[0:1] - top) for x in every]
        sums = sum(f * x[1:2] for f, x in zip(factors, every))
        delta = sum(f * x[2:3] for f, x in zip(factors, every)) / sums
        mine = jnp.exp(stat[c, k][0:1] - top) / sums
        sub = lax.broadcasted_iota(jnp.int32, (128, flat), 0)
        columns = jnp.where(sub == 0, mine, delta)
        sources = [stat[peer(n_col - d), k][0:1] for d in range(n_col)]
        for d, x in enumerate(sources):
            columns = jnp.where(sub == 2 + d, jnp.exp(x - top) / sums, columns)
        columns = columns.T
        for d in range(n_col):
            weight = columns[:, 2 + d : 3 + d].reshape(CHUNK, heads, 1) * own_mask[None]
            rows_here = pl.ds(pl.multiple_of(CHUNK * k, CHUNK), CHUNK)
            factor[d, rows_here, :] = jnp.sum(weight, axis=1)
        probs = s_ref[here].reshape(flat, -1) * columns[:, 0:1]
        ds = probs * (dp_ref[here].reshape(flat, -1) - columns[:, 1:2])
        ds = ds.reshape(CHUNK, heads, -1)
        dp_ref[here] = ds
        across = jnp.concatenate([ds[i] for i in range(CHUNK)], axis=1)
        x_hi, x_lo = split(pair_v[here].reshape(-1, channels))
        both = dot(stacked(across), jnp.concatenate([x_hi, x_lo], axis=1), NN)
        carry = carry + (
            both[:heads, :channels] + (both[:heads, channels:] + both[heads:, :channels])
        )
        return carry

    total_w[0] = in_pairs(0, n_chunk, backward, jnp.zeros((heads, channels), F32))
    near_copies = []
    for d in range(1, n_row):
        copy = remote(
            total_w.at[0], near.at[d], sum_send.at[d], sum_recv.at[d], row=(r + d) % n_row
        )
        copy.start()
        near_copies.append(copy)
    total = ctx_out[c] * factor[0]
    for d, copy in enumerate(ctx_copies, 1):
        copy.wait_recv()
        total = total + ctx_in[d] * factor[d]
    gctx[c] = total * gate_b[c]
    gctx_copies = spread_out(5, lambda d: gctx.at[c], lambda d: gctx.at[c])

    def pair_back(k, carry):
        ds = dp_ref[pl.ds(CHUNK * k, CHUNK)]
        columns = ds.reshape(flat, -1).T
        d_unit = dot_deep(columns, wide_b[...], wide_b[:flat])
        for i in range(CHUNK):
            d = d_unit[:, channels * i : channels * (i + 1)]
            x = pair_v[CHUNK * k + i]
            slope = jnp.sum(d * x, axis=-1, keepdims=True) * (1.0 / channels)
            grad_ref[CHUNK * k + i] = (d - x * slope) * scale_v[CHUNK * k + i]
        return carry

    in_pairs(0, n_chunk // 2, pair_back, 0)

    total = total_w[0]
    for d, copy in enumerate(near_copies, 1):
        copy.wait_recv()
        total = total + near[d]
    total_w[1] = total
    far_copies = []
    for d in range(1, n_col):
        k = n_row + d
        copy = remote(total_w.at[1], far.at[d], sum_send.at[k], sum_recv.at[k], col=peer(d))
        copy.start()
        far_copies.append(copy)
    in_pairs(n_chunk // 2, n_chunk, pair_back, 0)

    total = total_w[1]
    for d, copy in enumerate(far_copies, 1):
        copy.wait_recv()
        total = total + far[d]
    bgrad_ref[...] = total * pgain_ref[...]
    for copy in gctx_copies:
        copy.wait_recv()
    att_ref[...] = dot3(stacked(joined(gctx)), *split(wout_ref[...]), NT)

    waits = tok_copies + back_copies + back_copies2 + stat_copies + ctx_copies + gctx_copies
    for copy in waits + near_copies + far_copies:
        copy.wait_send()
    for condition, copy in forwards:
        if condition is None:
            copy.wait_send()
        else:
            pl.when(condition)(copy.wait_send)


def write_kernel(*refs):
    count = len(refs) // 2
    copies = [
        pltpu.make_async_copy(src, dst, refs[-1].at[k])
        for k, (src, dst) in enumerate(zip(refs[:count], refs[count:-1]))
    ]
    for copy in copies:
        copy.start()
    for copy in copies:
        copy.wait()


def local(
    n_row, n_col,
    single, pair, single_gain, pair_gain, w_query, w_key, w_value, w_gate, w_bias, w_out, cotangent
):
    tq, blk = single.shape
    width = single_gain.shape[0]
    channels, heads = w_bias.shape
    keys = pair.shape[1]
    n_chunk = tq // CHUNK
    vmem = pl.BlockSpec(memory_space=pltpu.VMEM)
    hbm = pl.BlockSpec(memory_space=pltpu.HBM)
    bits = (n_row // 2).bit_length() - 1
    w_bias_t = w_bias.T
    pair_gain = pair_gain.reshape(1, channels)
    blocks = pltpu.VMEM((n_col, tq, blk), F32)
    dma = pltpu.SemaphoreType.DMA
    attended, pair_grad, bias_grad = pl.pallas_call(
        functools.partial(layer_kernel, n_row, n_col, heads),
        out_shape=(
            pltpu.VMEM((tq, blk), F32),
            pltpu.VMEM(pair.shape, F32),
            pltpu.VMEM((heads, channels), F32),
        ),
        in_specs=[hbm] * 11,
        out_specs=(vmem,) * 3,
        scratch_shapes=[
            pltpu.VMEM(pair.shape, F32),
            pltpu.VMEM(pair.shape, F32),
            *[pltpu.VMEM((width, width), F32)] * 4,
            blocks,
            pltpu.VMEM((2, n_col, tq, blk), F32),
            blocks, blocks, blocks,
            pltpu.VMEM((tq, heads, keys), F32),
            pltpu.VMEM((tq, heads, keys), F32),
            pltpu.VMEM((tq, width), F32),
            pltpu.VMEM((tq, width), F32),
            blocks,
            *[pltpu.VMEM((2 * keys, width), BF16)] * 2,
            pltpu.VMEM((n_col, n_chunk, 8, CHUNK * heads), F32),
            pltpu.VMEM((tq, width), F32),
            blocks, blocks, blocks,
            *[pltpu.VMEM((4, width, width), BF16)] * 2,
            pltpu.VMEM((2 * CHUNK * heads, CHUNK * channels), BF16),
            pltpu.VMEM((2, heads, channels), F32),
            pltpu.VMEM((n_row, heads, channels), F32),
            pltpu.VMEM((n_col, heads, channels), F32),
            blocks,
            pltpu.VMEM((tq, blk), F32),
            pltpu.VMEM((blk, width), F32),
            pltpu.VMEM((heads, channels), F32),
            pltpu.VMEM((1, channels), F32),
            pltpu.VMEM((width,), F32),
            dma((6,)),
            dma((n_row + n_col,)), dma((n_row + n_col,)),
            dma((4,)), dma((n_chunk,)), dma((6, n_col)), dma((6, n_col)),
            dma((bits, n_col)), dma((n_col,)), dma((n_col,)), dma((n_col,)),
        ],
        compiler_params=pltpu.CompilerParams(
            collective_id=0, has_side_effects=True, vmem_limit_bytes=VMEM_LIMIT
        ),
        name="layer",
    )(
        *[
            pltpu.with_memory_space_constraint(x, pltpu.HBM)
            for x in (
                single, pair, single_gain, pair_gain, w_query, w_key, w_value, w_gate, w_bias_t,
                w_out.T, cotangent,
            )
        ]
    )
    results = (attended, pair_grad, bias_grad)
    attended, pair_grad, bias_grad = pl.pallas_call(
        write_kernel,
        out_shape=tuple(jax.ShapeDtypeStruct(x.shape, F32) for x in results),
        in_specs=[vmem] * 3,
        out_specs=(hbm,) * 3,
        scratch_shapes=[dma((3,))],
        compiler_params=pltpu.CompilerParams(vmem_limit_bytes=1024 * 1024),
        name="write_out",
    )(*[pltpu.with_memory_space_constraint(x, pltpu.VMEM) for x in results])
    return (attended, pair_grad, bias_grad.T)


def solution(mesh):
    placed = (
        P("row", "col"),
        P("row", "col", None),
        P(),
        P(),
        P(),
        P(),
        P(),
        P(),
        P(),
        P(None, "col"),
        P("row", "col"),
    )
    return jax.shard_map(
        functools.partial(local, mesh.shape["row"], mesh.shape["col"]),
        mesh=mesh,
        in_specs=placed,
        out_specs=(P("row", "col"), P("row", "col", None), P()),
        check_vma=False,
    )
```
